256 devices in a mesh: dp: 4 (over x), expert: 64 (over z, y, core).
Axes of the slice: x: 4, y: 4, z: 8, core: 2. Of those that a mesh axis runs over, the one named last changes fastest.
Arguments:
- tokens: bfloat16 [32768, 2048], P(('dp', 'expert')), may hold values from -6 to 6
- cotangent: bfloat16 [32768, 2048], P(('dp', 'expert')), may hold values from -6 to 6
- expert_ids: int32 [32768, 8], P(('dp', 'expert')), may hold values from 0 to 63, all different within a row
- combine: float32 [32768, 8], P(('dp', 'expert')), may hold values from 0.05 to 1
- capacity: int32 [64], replicated, may hold values from 4 to 8, as said below
- w_gate: bfloat16 [64, 2048, 384], P('expert', 'dp'), may hold values from -0.125 to 0.125
- w_up: bfloat16 [64, 2048, 384], P('expert', 'dp'), may hold values from -0.125 to 0.125
- w_down: bfloat16 [64, 384, 2048], P('expert', None, 'dp'), may hold values from -0.3125 to 0.3125
Outputs:
- mixed: bfloat16 [32768, 2048], P(('dp', 'expert'))
- grad_tokens: bfloat16 [32768, 2048], P(('dp', 'expert'))
- grad_combine: float32 [32768, 8], P(('dp', 'expert'))
- grad_gate: bfloat16 [64, 2048, 384], P('expert', 'dp')
- grad_up: bfloat16 [64, 2048, 384], P('expert', 'dp')
- grad_down: bfloat16 [64, 384, 2048], P('expert', None, 'dp')
The draws below stay inside these ranges and needn't reach their ends.
Inputs may be any that keep to these rules, and one draw needn't show every extreme that they name: Some expert has capacity 8 in every draw.
All inputs are finite; a program needn't handle non-finite values.
Results may differ from the reference program's by a relative error of at most 0.013.
Values may be sent and summed in bfloat16 or wider, within the bound.
No kernel may reach another device: no remote copies, remote signals or barrier semaphores. Data moves between devices by JAX's collectives and lax.ppermute only.
A program may use at most 64 MiB of HBM per device.

```python
import math
import jax
import jax.numpy as jnp
from jax import lax

D = 2048
FF = 384
TOP = 8
TOK_DEV = 128
EXPERTS = 64
CAP = 8
TOKENS = 32768
N_DP = 4
N_EXPERT = 64


def draw_capacity(key, part):
    key = jax.random.fold_in(key, 7)
    first_key, second_key = jax.random.split(key)
    lowest = max(1, CAP // 2)
    values = jax.random.randint(first_key, (EXPERTS,), lowest, CAP + lowest)
    values = jnp.minimum(values, CAP)
    chosen = jax.random.randint(second_key, (), 0, EXPERTS)
    return values.at[chosen].set(CAP).astype(jnp.int32)


def shard_levels(key, dims, cuts, low, high):
    def one(dim, shards_of):
        heights = jax.random.uniform(jax.random.fold_in(jax.random.fold_in(key, 6), dim), (shards_of,), jnp.float32, low / len(cuts), high / len(cuts))
        return jnp.repeat(jnp.exp(heights), dims[dim] // shards_of).reshape((-1,) + (1,) * (len(dims) - dim - 1))

    gain = one(*cuts[0])
    for cut in cuts[1:]:
        gain = gain * one(*cut)
    return gain


def distinct(key, rows, count, top, lift):
    order = jax.random.permutation(jax.random.fold_in(key, 1), count)
    favour = order
    for power in range(3):
        favour = favour * favour // count
    favour = favour * lift // count
    tickets = jax.random.randint(jax.random.fold_in(key, 2), (rows, count), 0, 4096) + favour
    fixed_rows = jax.random.permutation(jax.random.fold_in(key, 3), rows)[jnp.arange(count) % rows]
    tickets = jnp.where(jnp.arange(rows)[:, None] == fixed_rows[None, :], 1 << 14, tickets)
    merit = tickets * count + jnp.arange(count)
    return lax.top_k(merit.astype(jnp.int32), top)[1].astype(jnp.int32)


def scatter_about(key, extent, scale, most, cuts=(), kind=jnp.bfloat16):
    entries = scale * jax.random.normal(key, extent, jnp.float32)
    if cuts:
        entries = entries * shard_levels(key, extent, cuts, -0.22, 0.18)
    return jnp.clip(entries, -most, most).astype(kind)


def setup_inputs(seed: int = 0) -> dict:
    seeds = jax.random.split(jax.random.key(seed), 9)
    return {
        "tokens": scatter_about(seeds[0], (TOKENS, D), 1.0, 6.0, ((0, 256),)),
        "cotangent": scatter_about(seeds[1], (TOKENS, D), 1.0, 6.0, ((0, 256),)),
        "expert_ids": distinct(seeds[2], TOKENS, EXPERTS, TOP, 2048),
        "combine": jnp.clip(jnp.exp(math.log(1.0) - 2.9957323 * jax.random.uniform(seeds[3], (TOKENS, TOP), jnp.float32) ** shard_levels(seeds[3], (TOKENS, TOP), ((0, 256),), -0.2, 0.2)), 0.05, 1.0),
        "capacity": draw_capacity(jax.random.fold_in(seeds[8], 71), 0),
        "w_gate": scatter_about(seeds[5], (EXPERTS, D, FF), D ** -0.5, 0.125, ((0, 64), (1, 4))),
        "w_up": scatter_about(seeds[6], (EXPERTS, D, FF), D ** -0.5, 0.125, ((0, 64), (1, 4))),
        "w_down": scatter_about(seeds[7], (EXPERTS, FF, D), FF ** -0.5, 0.3125, ((0, 64), (2, 4))),
    }


def expert_math(rows, grads, wgate, wup, wdown):
    hidden_gate = jnp.dot(rows, wgate, preferred_element_type=jnp.float32)
    hidden_up = jnp.dot(rows, wup, preferred_element_type=jnp.float32)
    sigma = jax.nn.sigmoid(hidden_gate)
    active = (hidden_gate * sigma * hidden_up).astype(jnp.bfloat16)
    output = jnp.dot(active, wdown, preferred_element_type=jnp.float32).astype(jnp.bfloat16)
    d_active = jnp.dot(grads, wdown.T, preferred_element_type=jnp.float32)
    d_gate = (d_active * hidden_up * sigma * (1.0 + hidden_gate * (1.0 - sigma))).astype(jnp.bfloat16)
    d_up = (d_active * hidden_gate * sigma).astype(jnp.bfloat16)
    d_rows = (jnp.dot(d_gate, wgate.T, preferred_element_type=jnp.float32)
              + jnp.dot(d_up, wup.T, preferred_element_type=jnp.float32)).astype(jnp.bfloat16)
    return output, d_rows, active, d_gate, d_up


def group_sum(left, right):
    left_groups = left.astype(jnp.float32).reshape(N_DP, -1, left.shape[1])
    right_groups = right.astype(jnp.float32).reshape(N_DP, -1, right.shape[1])
    partial_sums = jnp.einsum("grn,grm->gnm", left_groups, right_groups)
    rounded = lax.optimization_barrier(partial_sums.astype(jnp.bfloat16))
    return jnp.sum(rounded.astype(jnp.float32), axis=0).astype(jnp.bfloat16)


def reference(tokens, cotangent, expert_ids, combine, capacity, w_gate, w_up, w_down):
    sources = N_DP * N_EXPERT
    assign_count = TOK_DEV * TOP
    ids = expert_ids.reshape(sources, assign_count)
    experts_all = jnp.arange(EXPERTS, dtype=jnp.int32)
    onehot = (ids[:, :, None] == experts_all[None, None, :]).astype(jnp.int32)
    ranking = jnp.sum((jnp.cumsum(onehot, axis=1) - onehot) * onehot, axis=2)
    limits = capacity[ids]
    position = jnp.where(ranking < limits, ids * CAP + ranking, EXPERTS * CAP).astype(jnp.int32)
    source_rows = jnp.arange(sources, dtype=jnp.int32)[:, None]
    filler = jnp.broadcast_to(jnp.arange(assign_count, dtype=jnp.int32)[None, :], (sources, assign_count))
    slot_table = jnp.full((sources, EXPERTS * CAP + 1), assign_count, jnp.int32)
    slot_table = slot_table.at[source_rows, position].set(filler)
    slot_table = slot_table[:, :EXPERTS * CAP].reshape(sources, EXPERTS, CAP)
    padded_tokens = jnp.concatenate(
        [tokens.reshape(sources, TOK_DEV, D), jnp.zeros((sources, 1, D), jnp.bfloat16)], axis=1)
    padded_grads = jnp.concatenate(
        [cotangent.reshape(sources, TOK_DEV, D), jnp.zeros((sources, 1, D), jnp.bfloat16)], axis=1)
    padded_weights = jnp.concatenate(
        [combine.reshape(sources, assign_count), jnp.zeros((sources, 1), jnp.float32)], axis=1)

    def per_expert(totals, expert_index):
        mixed_sum, dx_sum, weight_sum = totals
        assigned = lax.dynamic_index_in_dim(slot_table, expert_index, 1, keepdims=False)
        token_index = (assigned // TOP).astype(jnp.int32)
        rows = jnp.take_along_axis(padded_tokens, token_index[:, :, None], axis=1)
        raw_grads = jnp.take_along_axis(padded_grads, token_index[:, :, None], axis=1)
        weights = jnp.take_along_axis(padded_weights, assigned, axis=1)
        scaled = (weights[:, :, None] * raw_grads.astype(jnp.float32)).astype(jnp.bfloat16)
        wgate = lax.dynamic_index_in_dim(w_gate, expert_index, 0, keepdims=False)
        wup = lax.dynamic_index_in_dim(w_up, expert_index, 0, keepdims=False)
        wdown = lax.dynamic_index_in_dim(w_down, expert_index, 0, keepdims=False)
        flat_rows = rows.reshape(-1, D)
        flat_scaled = scaled.reshape(-1, D)
        output, d_rows, active, d_gate, d_up = expert_math(flat_rows, flat_scaled, wgate, wup, wdown)
        output_blocks = output.reshape(sources, CAP, D).astype(jnp.float32)
        mixed_sum = mixed_sum.at[source_rows, token_index].add(weights[:, :, None] * output_blocks)
        dx_sum = dx_sum.at[source_rows, token_index].add(d_rows.reshape(sources, CAP, D).astype(jnp.float32))
        weight_sum = weight_sum.at[source_rows, assigned].add(
            jnp.sum(raw_grads.astype(jnp.float32) * output_blocks, axis=2))
        grads = (group_sum(flat_rows, d_gate), group_sum(flat_rows, d_up), group_sum(active, flat_scaled))
        return (mixed_sum, dx_sum, weight_sum), grads

    start = (jnp.zeros((sources, TOK_DEV + 1, D), jnp.float32),
             jnp.zeros((sources, TOK_DEV + 1, D), jnp.float32),
             jnp.zeros((sources, assign_count + 1), jnp.float32))
    totals, grads = lax.scan(per_expert, start, experts_all)
    mixed = totals[0][:, :TOK_DEV].reshape(TOKENS, D).astype(jnp.bfloat16)
    grad_tokens = totals[1][:, :TOK_DEV].reshape(TOKENS, D).astype(jnp.bfloat16)
    grad_combine = totals[2][:, :assign_count].reshape(TOKENS, TOP)
    return mixed, grad_tokens, grad_combine, grads[0], grads[1], grads[2]
```

```python
import functools

import jax
import jax.numpy as jnp
from jax import lax
from jax.experimental import pallas as pl
from jax.experimental.pallas import tpu as pltpu
from jax.sharding import PartitionSpec as P

VMEM_LIMIT = 48 * 2**20
BF = jnp.bfloat16
F32 = jnp.float32


def contract(left, right, left_dim, right_dim):
    return lax.dot_general(
        left, right, (((left_dim,), (right_dim,)), ((), ())), preferred_element_type=F32
    )


def call(body, name, out_shape, args, flops):
    outs = out_shape if isinstance(out_shape, (tuple, list)) else [out_shape]
    moved = sum(a.size * a.dtype.itemsize for a in (*args, *outs))
    return pl.pallas_call(
        body,
        out_shape=out_shape,
        name=name,
        compiler_params=pltpu.CompilerParams(vmem_limit_bytes=VMEM_LIMIT),
        cost_estimate=pl.CostEstimate(flops=flops, bytes_accessed=moved, transcendentals=0),
    )(*args)


def routing(ids, capacity, slots):
    count, top = ids.shape
    lanes = lax.broadcasted_iota(jnp.int32, (count, 128), 1)
    chosen = jnp.zeros((count, 128), F32)
    for k in range(top):
        chosen = chosen + (ids[:, k : k + 1] == lanes).astype(F32)
    earlier = (
        lax.broadcasted_iota(jnp.int32, (count, count), 1)
        < lax.broadcasted_iota(jnp.int32, (count, count), 0)
    ).astype(BF)
    rank = contract(earlier, chosen.astype(BF), 1, 0)
    kept = (chosen > 0.5) & (rank < capacity.astype(F32))
    slot = jnp.where(kept, rank, -1.0)
    return slot.T


def one_hot(slot_of, experts, slots):
    count = slot_of.shape[1]
    wanted = lax.broadcasted_iota(jnp.int32, (experts, slots, count), 1).astype(F32)
    held = jnp.broadcast_to(slot_of[:experts, None, :], (experts, slots, count))
    return (held == wanted).astype(F32).reshape(experts * slots, count)


def weight_of(ids, combine):
    count, top = ids.shape
    lanes = lax.broadcasted_iota(jnp.int32, (count, 128), 1)
    weights = jnp.zeros((count, 128), F32)
    for k in range(top):
        weights = weights + jnp.where(ids[:, k : k + 1] == lanes, combine[:, k : k + 1], 0.0)
    return weights.T


def spread(weights, experts, slots):
    count = weights.shape[1]
    return jnp.broadcast_to(weights[:experts, None, :], (experts, slots, count)).reshape(
        experts * slots, count
    )


def pick_tokens(experts, slots, ids_ref, cap_ref, tokens_ref, out_ref):
    slot_of = routing(ids_ref[...], cap_ref[...], slots)
    pick = one_hot(slot_of, experts, slots).astype(BF)
    width = tokens_ref.shape[1]
    for c in range(0, width, 512):
        out_ref[:, c : c + 512] = contract(pick, tokens_ref[:, c : c + 512], 1, 0).astype(BF)


def pick_scaled(experts, slots, ids_ref, cap_ref, comb_ref, cot_ref, out_ref):
    slot_of = routing(ids_ref[...], cap_ref[...], slots)
    held = one_hot(slot_of, experts, slots)
    weights = spread(weight_of(ids_ref[...], comb_ref[...]), experts, slots)
    scale = jnp.sum(held * weights, axis=1, keepdims=True)
    pick = held.astype(BF)
    width = cot_ref.shape[1]
    for c in range(0, width, 512):
        rows = contract(pick, cot_ref[:, c : c + 512], 1, 0)
        out_ref[:, c : c + 512] = (scale * rows).astype(BF)


def forward(x_ref, wg_ref, wu_ref, wd_ref, o_ref, h_ref, u_ref, a_ref):
    x = x_ref[...]
    h = contract(x, wg_ref[...], 1, 0)
    u = contract(x, wu_ref[...], 1, 0)
    a = (h * jax.nn.sigmoid(h) * u).astype(BF)
    h_ref[...] = h
    u_ref[...] = u
    a_ref[...] = a
    width = o_ref.shape[1]
    for c in range(0, width, 512):
        o_ref[:, c : c + 512] = contract(a, wd_ref[:, c : c + 512], 1, 0).astype(BF)


def backward(g_ref, h_ref, u_ref, wg_ref, wu_ref, wd_ref, dx_ref, dh_ref, du_ref):
    da = contract(g_ref[...], wd_ref[...], 1, 1)
    h = h_ref[...]
    s = jax.nn.sigmoid(h)
    dh = (da * u_ref[...] * s * (1.0 + h * (1.0 - s))).astype(BF)
    du = (da * h * s).astype(BF)
    dh_ref[...] = dh
    du_ref[...] = du
    width = dx_ref.shape[1]
    for c in range(0, width, 512):
        dx_ref[:, c : c + 512] = (
            contract(dh, wg_ref[c : c + 512, :], 1, 1) + contract(du, wu_ref[c : c + 512, :], 1, 1)
        ).astype(BF)


def weight_grads(x_ref, g_ref, a_ref, dh_ref, du_ref, gg_ref, gu_ref, gd_ref):
    width = x_ref.shape[1]
    dh, du, a = dh_ref[...], du_ref[...], a_ref[...]
    for c in range(0, width, 512):
        x = x_ref[:, c : c + 512]
        gg_ref[c : c + 512, :] = contract(x, dh, 0, 0).astype(BF)
        gu_ref[c : c + 512, :] = contract(x, du, 0, 0).astype(BF)
        gd_ref[:, c : c + 512] = contract(a, g_ref[:, c : c + 512], 0, 0).astype(BF)


def merge_outputs(experts, slots, ids_ref, cap_ref, comb_ref, cot_ref, o_ref, mixed_ref, gc_ref):
    ids = ids_ref[...]
    count, top = ids.shape
    slot_of = routing(ids, cap_ref[...], slots)
    held = one_hot(slot_of, experts, slots)
    weights = spread(weight_of(ids, comb_ref[...]), experts, slots)
    share = held * weights
    high = share.astype(BF)
    low = (share - high.astype(F32)).astype(BF)
    width = o_ref.shape[1]
    dots = jnp.zeros(share.shape, F32)
    for c in range(0, width, 512):
        o = o_ref[:, c : c + 512]
        mixed_ref[:, c : c + 512] = (contract(high, o, 0, 0) + contract(low, o, 0, 0)).astype(BF)
        dots = dots + contract(o, cot_ref[:, c : c + 512], 1, 1)
    per_expert = jnp.sum((held * dots).reshape(experts, slots, count), axis=1)
    pad = jnp.zeros((128 - experts, count), F32)
    by_token = jnp.concatenate([per_expert, pad], axis=0).T
    lanes = lax.broadcasted_iota(jnp.int32, (count, 128), 1)
    for k in range(top):
        gc_ref[:, k : k + 1] = jnp.sum(
            jnp.where(ids[:, k : k + 1] == lanes, by_token, 0.0), axis=1, keepdims=True
        )


def merge_rows(experts, slots, ids_ref, cap_ref, dx_ref, out_ref):
    slot_of = routing(ids_ref[...], cap_ref[...], slots)
    pick = one_hot(slot_of, experts, slots).astype(BF)
    width = dx_ref.shape[1]
    for c in range(0, width, 512):
        out_ref[:, c : c + 512] = contract(pick, dx_ref[:, c : c + 512], 0, 0).astype(BF)


def on_device(tokens, cotangent, expert_ids, combine, capacity, w_gate, w_up, w_down):
    peers = lax.axis_size("expert")
    count, width = tokens.shape
    top = expert_ids.shape[1]
    experts = capacity.shape[0]
    slots = count * top // (2 * peers)
    rows = experts * slots
    hidden = w_gate.shape[2]
    limits = jnp.pad(capacity, (0, 128 - experts)).reshape(1, 128)
    ids = expert_ids
    of = jax.ShapeDtypeStruct
    unit = 2 * rows * width * hidden
    pick_flops = 2 * rows * count * width

    def exchange(x):
        x = x.reshape(peers, slots, width)
        return lax.all_to_all(x, "expert", 0, 0, tiled=True).reshape(rows, width)

    part = functools.partial
    sent_x = call(part(pick_tokens, experts, slots), "pick_tokens", of((rows, width), BF), (ids, limits, tokens), pick_flops)
    x = exchange(sent_x)
    sent_g = call(part(pick_scaled, experts, slots), "pick_scaled", of((rows, width), BF), (ids, limits, combine, cotangent), pick_flops)
    wg = lax.all_gather(w_gate[0], "dp", axis=0, tiled=True)
    wu = lax.all_gather(w_up[0], "dp", axis=0, tiled=True)
    wd = lax.all_gather(w_down[0], "dp", axis=1, tiled=True)
    g = exchange(sent_g)
    o, h, u, a = call(
        forward, "forward",
        [of((rows, width), BF), of((rows, hidden), F32), of((rows, hidden), F32), of((rows, hidden), BF)],
        (x, wg, wu, wd), 3 * unit,
    )
    back_o = exchange(o)
    dx, dh, du = call(
        backward, "backward",
        [of((rows, width), BF), of((rows, hidden), BF), of((rows, hidden), BF)],
        (g, h, u, wg, wu, wd), 3 * unit,
    )
    back_dx = exchange(dx)
    gg, gu, gd = call(
        weight_grads, "weight_grads",
        [of((width, hidden), BF), of((width, hidden), BF), of((hidden, width), BF)],
        (x, g, a, dh, du), 3 * unit,
    )
    grad_gate = lax.psum_scatter(gg, "dp", scatter_dimension=0, tiled=True)
    grad_up = lax.psum_scatter(gu, "dp", scatter_dimension=0, tiled=True)
    grad_down = lax.psum_scatter(gd, "dp", scatter_dimension=1, tiled=True)
    mixed, grad_combine = call(
        part(merge_outputs, experts, slots), "merge_outputs",
        [of((count, width), BF), of((count, top), F32)],
        (ids, limits, combine, cotangent, back_o), 3 * pick_flops,
    )
    grad_tokens = call(
        part(merge_rows, experts, slots), "merge_rows", of((count, width), BF), (ids, limits, back_dx), pick_flops
    )
    return (mixed, grad_tokens, grad_combine, grad_gate[None], grad_up[None], grad_down[None])


def solution(mesh):
    rows = P(("dp", "expert"), None)
    return jax.shard_map(
        on_device,
        mesh=mesh,
        in_specs=(rows, rows, rows, rows, P(), P("expert", "dp", None), P("expert", "dp", None), P("expert", None, "dp")),
        out_specs=(rows, rows, rows, P("expert", "dp", None), P("expert", "dp", None), P("expert", None, "dp")),
        check_vma=False,
    )
```

```python
import functools

import jax
import jax.numpy as jnp
from jax import lax
from jax.experimental import pallas as pl
from jax.experimental.pallas import tpu as pltpu
from jax.sharding import PartitionSpec as P

VMEM_LIMIT = 48 * 2**20
BF = jnp.bfloat16
F32 = jnp.float32


def contract(left, right, left_dim, right_dim):
    return lax.dot_general(
        left, right, (((left_dim,), (right_dim,)), ((), ())), preferred_element_type=F32
    )


def call(body, name, out_shape, args, flops):
    outs = out_shape if isinstance(out_shape, (tuple, list)) else [out_shape]
    moved = sum(a.size * a.dtype.itemsize for a in (*args, *outs))
    return pl.pallas_call(
        body,
        out_shape=out_shape,
        name=name,
        compiler_params=pltpu.CompilerParams(vmem_limit_bytes=VMEM_LIMIT),
        cost_estimate=pl.CostEstimate(flops=flops, bytes_accessed=moved, transcendentals=0),
    )(*args)


def routing(ids, capacity, slots):
    count, top = ids.shape
    lanes = lax.broadcasted_iota(jnp.int32, (count, 128), 1)
    chosen = jnp.zeros((count, 128), F32)
    for k in range(top):
        chosen = chosen + (ids[:, k : k + 1] == lanes).astype(F32)
    earlier = (
        lax.broadcasted_iota(jnp.int32, (count, count), 1)
        < lax.broadcasted_iota(jnp.int32, (count, count), 0)
    ).astype(BF)
    rank = contract(earlier, chosen.astype(BF), 1, 0)
    kept = (chosen > 0.5) & (rank < capacity.astype(F32))
    slot = jnp.where(kept, rank, -1.0)
    return slot.T


def one_hot(slot_of, experts, slots):
    count = slot_of.shape[1]
    wanted = lax.broadcasted_iota(jnp.int32, (experts, slots, count), 1).astype(F32)
    held = jnp.broadcast_to(slot_of[:experts, None, :], (experts, slots, count))
    return (held == wanted).astype(F32).reshape(experts * slots, count)


def weight_of(ids, combine):
    count, top = ids.shape
    lanes = lax.broadcasted_iota(jnp.int32, (count, 128), 1)
    weights = jnp.zeros((count, 128), F32)
    for k in range(top):
        weights = weights + jnp.where(ids[:, k : k + 1] == lanes, combine[:, k : k + 1], 0.0)
    return weights.T


def spread(weights, experts, slots):
    count = weights.shape[1]
    return jnp.broadcast_to(weights[:experts, None, :], (experts, slots, count)).reshape(
        experts * slots, count
    )


def pick_rows(experts, slots, ids_ref, cap_ref, comb_ref, tokens_ref, cot_ref, out_ref):
    slot_of = routing(ids_ref[...], cap_ref[...], slots)
    held = one_hot(slot_of, experts, slots)
    weights = spread(weight_of(ids_ref[...], comb_ref[...]), experts, slots)
    scale = jnp.sum(held * weights, axis=1, keepdims=True)
    pick = held.astype(BF)
    width = tokens_ref.shape[1]
    for c in range(0, width, 512):
        out_ref[:, c : c + 512] = contract(pick, tokens_ref[:, c : c + 512], 1, 0).astype(BF)
    for c in range(0, width, 512):
        rows = contract(pick, cot_ref[:, c : c + 512], 1, 0)
        out_ref[:, width + c : width + c + 512] = (scale * rows).astype(BF)


def expert_math(xg_ref, wg_ref, wu_ref, wd_ref, od_ref, a_ref, dh_ref, du_ref):
    width = wg_ref.shape[0]
    x = xg_ref[:, :width]
    h = contract(x, wg_ref[...], 1, 0)
    u = contract(x, wu_ref[...], 1, 0)
    s = jax.nn.sigmoid(h)
    a = (h * s * u).astype(BF)
    a_ref[...] = a
    for c in range(0, width, 512):
        od_ref[:, c : c + 512] = contract(a, wd_ref[:, c : c + 512], 1, 0).astype(BF)
    da = contract(xg_ref[:, width:], wd_ref[...], 1, 1)
    dh = (da * u * s * (1.0 + h * (1.0 - s))).astype(BF)
    du = (da * h * s).astype(BF)
    dh_ref[...] = dh
    du_ref[...] = du
    for c in range(0, width, 512):
        od_ref[:, width + c : width + c + 512] = (
            contract(dh, wg_ref[c : c + 512, :], 1, 1) + contract(du, wu_ref[c : c + 512, :], 1, 1)
        ).astype(BF)


def weight_grads(xg_ref, a_ref, dh_ref, du_ref, gg_ref, gu_ref, gd_ref):
    width = gg_ref.shape[0]
    dh, du, a = dh_ref[...], du_ref[...], a_ref[...]
    for c in range(0, width, 512):
        x = xg_ref[:, c : c + 512]
        gg_ref[c : c + 512, :] = contract(x, dh, 0, 0).astype(BF)
        gu_ref[c : c + 512, :] = contract(x, du, 0, 0).astype(BF)
        gd_ref[:, c : c + 512] = contract(a, xg_ref[:, width + c : width + c + 512], 0, 0).astype(BF)


def merge(experts, slots, ids_ref, cap_ref, comb_ref, cot_ref, od_ref, mixed_ref, rows_ref, gc_ref):
    ids = ids_ref[...]
    count, top = ids.shape
    slot_of = routing(ids, cap_ref[...], slots)
    held = one_hot(slot_of, experts, slots)
    weights = spread(weight_of(ids, comb_ref[...]), experts, slots)
    share = held * weights
    high = share.astype(BF)
    low = (share - high.astype(F32)).astype(BF)
    width = cot_ref.shape[1]
    dots = jnp.zeros(share.shape, F32)
    for c in range(0, width, 512):
        o = od_ref[:, c : c + 512]
        mixed_ref[:, c : c + 512] = (contract(high, o, 0, 0) + contract(low, o, 0, 0)).astype(BF)
        dots = dots + contract(o, cot_ref[:, c : c + 512], 1, 1)
    pick = held.astype(BF)
    for c in range(0, width, 512):
        rows_ref[:, c : c + 512] = contract(pick, od_ref[:, width + c : width + c + 512], 0, 0).astype(BF)
    per_expert = jnp.sum((held * dots).reshape(experts, slots, count), axis=1)
    pad = jnp.zeros((128 - experts, count), F32)
    by_token = jnp.concatenate([per_expert, pad], axis=0).T
    lanes = lax.broadcasted_iota(jnp.int32, (count, 128), 1)
    for k in range(top):
        gc_ref[:, k : k + 1] = jnp.sum(
            jnp.where(ids[:, k : k + 1] == lanes, by_token, 0.0), axis=1, keepdims=True
        )


def on_device(tokens, cotangent, expert_ids, combine, capacity, w_gate, w_up, w_down):
    peers = lax.axis_size("expert")
    count, width = tokens.shape
    top = expert_ids.shape[1]
    experts = capacity.shape[0]
    slots = count * top // (2 * peers)
    rows = experts * slots
    hidden = w_gate.shape[2]
    limits = jnp.pad(capacity, (0, 128 - experts)).reshape(1, 128)
    ids = expert_ids
    of = jax.ShapeDtypeStruct
    unit = 2 * rows * width * hidden
    pick_flops = 2 * rows * count * width

    def exchange(x):
        x = x.reshape(peers, slots, 2 * width)
        return lax.all_to_all(x, "expert", 0, 0, tiled=True).reshape(rows, 2 * width)

    part = functools.partial
    sent = call(
        part(pick_rows, experts, slots), "pick_rows", of((rows, 2 * width), BF),
        (ids, limits, combine, tokens, cotangent), 2 * pick_flops,
    )
    xg = exchange(sent)
    wg = lax.all_gather(w_gate[0], "dp", axis=0, tiled=True)
    wu = lax.all_gather(w_up[0], "dp", axis=0, tiled=True)
    wd = lax.all_gather(w_down[0], "dp", axis=1, tiled=True)
    od, a, dh, du = call(
        expert_math, "expert_math",
        [of((rows, 2 * width), BF), of((rows, hidden), BF), of((rows, hidden), BF), of((rows, hidden), BF)],
        (xg, wg, wu, wd), 6 * unit,
    )
    back = exchange(od)
    gg, gu, gd = call(
        weight_grads, "weight_grads",
        [of((width, hidden), BF), of((width, hidden), BF), of((hidden, width), BF)],
        (xg, a, dh, du), 3 * unit,
    )
    grad_gate = lax.psum_scatter(gg, "dp", scatter_dimension=0, tiled=True)
    grad_up = lax.psum_scatter(gu, "dp", scatter_dimension=0, tiled=True)
    grad_down = lax.psum_scatter(gd, "dp", scatter_dimension=1, tiled=True)
    mixed, grad_tokens, grad_combine = call(
        part(merge, experts, slots), "merge",
        [of((count, width), BF), of((count, width), BF), of((count, top), F32)],
        (ids, limits, combine, cotangent, back), 4 * pick_flops,
    )
    return (mixed, grad_tokens, grad_combine, grad_gate[None], grad_up[None], grad_down[None])


def solution(mesh):
    rows = P(("dp", "expert"), None)
    return jax.shard_map(
        on_device,
        mesh=mesh,
        in_specs=(rows, rows, rows, rows, P(), P("expert", "dp", None), P("expert", "dp", None), P("expert", None, "dp")),
        out_specs=(rows, rows, rows, P("expert", "dp", None), P("expert", "dp", None), P("expert", None, "dp")),
        check_vma=False,
    )
```

```python
import functools

import jax
import jax.numpy as jnp
from jax import lax
from jax.experimental import pallas as pl
from jax.experimental.pallas import tpu as pltpu
from jax.sharding import Mesh, PartitionSpec as P

VMEM_LIMIT = 48 * 2**20
BF = jnp.bfloat16
F32 = jnp.float32
STEP = 512


def contract(left, right, left_dim, right_dim):
    return lax.dot_general(
        left, right, (((left_dim,), (right_dim,)), ((), ())), preferred_element_type=F32
    )


def call(body, name, out_shape, args, flops, scalar=False):
    outs = out_shape if isinstance(out_shape, (tuple, list)) else [out_shape]
    moved = sum(a.size * a.dtype.itemsize for a in (*args, *outs))
    specs = [pl.BlockSpec(memory_space=pltpu.VMEM) for _ in args]
    if scalar:
        specs[0] = pl.BlockSpec(memory_space=pltpu.SMEM)
    return pl.pallas_call(
        body,
        out_shape=out_shape,
        in_specs=specs,
        name=name,
        compiler_params=pltpu.CompilerParams(vmem_limit_bytes=VMEM_LIMIT),
        cost_estimate=pl.CostEstimate(flops=flops, bytes_accessed=moved, transcendentals=0),
    )(*args)


def route(experts, ids_ref, cap_ref, comb_ref, out_ref):
    ids = ids_ref[...]
    comb = comb_ref[...]
    count, top = ids.shape
    lanes = lax.broadcasted_iota(jnp.int32, (count, 128), 1)
    chosen = jnp.zeros((count, 128), F32)
    weights = jnp.zeros((count, 128), F32)
    for k in range(top):
        hit = ids[:, k : k + 1] == lanes
        chosen = chosen + hit.astype(F32)
        weights = weights + jnp.where(hit, comb[:, k : k + 1], 0.0)
    earlier = (
        lax.broadcasted_iota(jnp.int32, (count, count), 1)
        < lax.broadcasted_iota(jnp.int32, (count, count), 0)
    ).astype(BF)
    rank = contract(earlier, chosen.astype(BF), 1, 0)
    kept = (chosen > 0.5) & (rank < cap_ref[...].astype(F32))
    out_ref[:experts, :] = jnp.where(kept, rank, -1.0).T[:experts]
    out_ref[experts:, :] = weights.T[:experts]


def plane_hits(z_ref, routes_ref, offset, peers, slots):
    planes, both, count = routes_ref.shape
    z = z_ref[0]
    source = lax.rem(z + offset + planes, planes)
    first = pl.multiple_of(z * peers, 8)
    slot_of = routes_ref[source, pl.ds(first, peers), :]
    weight = routes_ref[source, pl.ds(both // 2 + first, peers), :]
    wanted = lax.broadcasted_iota(jnp.int32, (peers, slots, count), 1).astype(F32)
    held = (jnp.broadcast_to(slot_of[:, None, :], (peers, slots, count)) == wanted).astype(F32)
    held = held.reshape(peers * slots, count)
    weight = jnp.broadcast_to(weight[:, None, :], (peers, slots, count)).reshape(peers * slots, count)
    return held, held * weight


def columns(refs, c):
    if len(refs) == 1:
        return refs[0][:, c : c + STEP]
    return jnp.concatenate([r[:, c : c + STEP] for r in refs], axis=0)


def pick_rows(offsets, pieces, z_ref, routes_ref, *refs):
    out_ref = refs[-1]
    peers, _, slots, double = out_ref.shape
    width = double // 2
    for j, offset in enumerate(offsets):
        x_refs = refs[j * pieces : (j + 1) * pieces]
        g_refs = refs[(len(offsets) + j) * pieces : (len(offsets) + j + 1) * pieces]
        held, share = plane_hits(z_ref, routes_ref, offset, peers, slots)
        scale = jnp.sum(share, axis=1, keepdims=True)
        pick = held.astype(BF)
        for c in range(0, width, STEP):
            rows = contract(pick, columns(x_refs, c), 1, 0)
            out_ref[:, j, :, c : c + STEP] = rows.reshape(peers, slots, STEP).astype(BF)
            rows = scale * contract(pick, columns(g_refs, c), 1, 0)
            out_ref[:, j, :, width + c : width + c + STEP] = rows.reshape(peers, slots, STEP).astype(BF)


def expert_math(xg_ref, w_ref, od_ref, a_ref, dh_ref, du_ref):
    parts, _, deep, _ = w_ref.shape
    width = parts * deep

    def over_width(start, which):
        return sum(
            contract(xg_ref[:, start + d * deep : start + (d + 1) * deep], w_ref[d, which], 1, 0)
            for d in range(parts)
        )

    h = over_width(0, 0)
    u = over_width(0, 1)
    s = jax.nn.sigmoid(h)
    a = (h * s * u).astype(BF)
    a_ref[...] = a
    for d in range(parts):
        od_ref[:, d * deep : (d + 1) * deep] = contract(a, w_ref[d, 2], 1, 1).astype(BF)
    da = over_width(width, 2)
    dh = (da * u * s * (1.0 + h * (1.0 - s))).astype(BF)
    du = (da * h * s).astype(BF)
    dh_ref[...] = dh
    du_ref[...] = du
    for d in range(parts):
        od_ref[:, width + d * deep : width + (d + 1) * deep] = (
            contract(dh, w_ref[d, 0], 1, 1) + contract(du, w_ref[d, 1], 1, 1)
        ).astype(BF)


def weight_grads(groups, *refs):
    xg, a, dh, du = (refs[i * groups : (i + 1) * groups] for i in range(4))
    out_ref = refs[-1]
    parts, _, deep, _ = out_ref.shape
    width = parts * deep
    a, dh, du = (jnp.concatenate([r[...] for r in rs], axis=0) for rs in (a, dh, du))
    for d in range(parts):
        x = jnp.concatenate([r[:, d * deep : (d + 1) * deep] for r in xg], axis=0)
        out_ref[d, 0] = contract(x, dh, 0, 0).astype(BF)
        out_ref[d, 1] = contract(x, du, 0, 0).astype(BF)
        g = jnp.concatenate([r[:, width + d * deep : width + (d + 1) * deep] for r in xg], axis=0)
        out_ref[d, 2] = contract(g, a, 0, 0).astype(BF)


def combine_grads(offsets, pieces, z_ref, routes_ref, back_ref, *refs):
    out_ref = refs[-1]
    peers, _, slots, double = back_ref.shape
    width = double // 2
    for j, offset in enumerate(offsets):
        g_refs = refs[j * pieces : (j + 1) * pieces]
        held, _ = plane_hits(z_ref, routes_ref, offset, peers, slots)
        dots = jnp.zeros(held.shape, F32)
        for c in range(0, width, STEP):
            rows = back_ref[:, j, :, c : c + STEP].astype(F32).reshape(peers * slots, STEP).astype(BF)
            dots = dots + contract(rows, columns(g_refs, c), 1, 1)
        out_ref[j] = jnp.sum((held * dots).reshape(peers, slots, -1), axis=1)


def fold(wanted, outputs, shape_of, z_ref, routes_ref, back_ref, *refs):
    peers, _, slots, double = back_ref.shape
    width = double // 2
    start = 0 if outputs else width
    count = routes_ref.shape[2]
    half = count // 2
    received = refs[: len(refs) - shape_of]
    out_refs = refs[len(refs) - shape_of :]
    for i, (offset, j, low_in, high_in) in enumerate(wanted):
        held, share = plane_hits(z_ref, routes_ref, offset, peers, slots)
        high = (share if outputs else held).astype(BF)
        if outputs:
            low = (share - high.astype(F32)).astype(BF)
        for c in range(0, width, STEP):
            rows = back_ref[:, j, :, start + c : start + c + STEP]
            rows = rows.astype(F32).reshape(peers * slots, STEP).astype(BF)
            total = contract(high, rows, 0, 0)
            if outputs:
                total = total + contract(low, rows, 0, 0)
            lower, upper = total[:half], total[half:]
            for n, whole in low_in:
                lower = lower + received[n][:half, c : c + STEP].astype(F32)
            for n, whole in high_in:
                piece = received[n][half:, c : c + STEP] if whole else received[n][:, c : c + STEP]
                upper = upper + piece.astype(F32)
            if shape_of > len(wanted):
                out_refs[0][:, c : c + STEP] = lower.astype(BF)
                out_refs[1][:, c : c + STEP] = upper.astype(BF)
            else:
                out_refs[i][:half, c : c + STEP] = lower.astype(BF)
                out_refs[i][half:, c : c + STEP] = upper.astype(BF)


def by_choice(ids_ref, grads_ref, out_ref):
    ids = ids_ref[...]
    count, top = ids.shape
    experts = grads_ref.shape[0]
    pad = jnp.zeros((128 - experts, count), F32)
    by_token = jnp.concatenate([grads_ref[...], pad], axis=0).T
    lanes = lax.broadcasted_iota(jnp.int32, (count, 128), 1)
    for k in range(top):
        out_ref[:, k : k + 1] = jnp.sum(
            jnp.where(ids[:, k : k + 1] == lanes, by_token, 0.0), axis=1, keepdims=True
        )


def on_device(tokens, cotangent, ids, combine, capacity, w_gate, w_up, w_down):
    part = functools.partial
    of = jax.ShapeDtypeStruct
    planes = lax.axis_size("z")
    peers = lax.axis_size("y") * lax.axis_size("core")
    count, width = tokens.shape
    top = ids.shape[1]
    experts = capacity.shape[0]
    slots = count * top // (2 * experts)
    hidden = w_gate.shape[2]
    half = count // 2
    far = planes // 2
    limits = jnp.pad(capacity, (0, 128 - experts)).reshape(1, 128)
    z = lax.axis_index("z").astype(jnp.int32).reshape(1)

    def up(x):
        return lax.ppermute(x, "z", [(i, (i + 1) % planes) for i in range(planes)])

    def down(x):
        return lax.ppermute(x, "z", [(i, (i - 1) % planes) for i in range(planes)])

    def across(x):
        return lax.all_to_all(x, ("y", "core"), 0, 0, tiled=True)

    mine = call(part(route, experts), "route", of((2 * experts, count), F32), (ids, limits, combine), 2 * count * count * 128)
    routes = lax.all_gather(mine, "z", axis=0, tiled=False)
    stacked = jnp.stack([w_gate[0], w_up[0], w_down[0].T])
    weights = lax.all_gather(stacked, "dp", axis=0, tiled=False)

    sources = {0: ([tokens], [cotangent])}
    x_up = x_down = tokens
    g_up = g_down = cotangent
    for step in range(1, far):
        x_up, x_down = up(x_up), down(x_down)
        g_up, g_down = up(g_up), down(g_down)
        sources[-step] = ([x_up], [g_up])
        sources[step] = ([x_down], [g_down])
    sources[far] = (
        [up(x_up[:half]), down(x_down[half:])],
        [up(g_up[:half]), down(g_down[half:])],
    )
    groups = [[0, -1, 1]] + [[-s, s] for s in range(2, far)] + [[far]]

    unit = 2 * peers * slots * width * hidden
    pick_flops = 2 * peers * slots * count * width
    xg, a, dh, du, back, grads = [], [], [], [], [], {}
    for offsets in groups:
        n = len(offsets)
        pieces = len(sources[offsets[0]][0])
        xs = [p for o in offsets for p in sources[o][0]]
        gs = [p for o in offsets for p in sources[o][1]]
        sent = call(
            part(pick_rows, offsets, pieces), "pick_rows", of((peers, n, slots, 2 * width), BF),
            (z, routes, *xs, *gs), 2 * n * pick_flops, True,
        )
        rows = n * peers * slots
        xg.append(across(sent).reshape(rows, 2 * width))
        od, *saved = call(
            expert_math, "expert_math",
            [of((rows, 2 * width), BF)] + [of((rows, hidden), BF)] * 3,
            (xg[-1], weights), 6 * n * unit,
        )
        for kept, new in zip((a, dh, du), saved):
            kept.append(new)
        back.append(across(od.reshape(peers, n, slots, 2 * width)))
        found = call(
            part(combine_grads, offsets, pieces), "combine_grads", of((n, peers, count), F32),
            (z, routes, back[-1], *gs), n * pick_flops, True,
        )
        for i, offset in enumerate(offsets):
            grads[offset % planes] = found[i]
    partial_grads = call(
        part(weight_grads, len(groups)), "weight_grads", of(weights.shape, BF),
        (*xg, *a, *dh, *du), 3 * planes * unit,
    )
    summed = lax.psum_scatter(partial_grads, "dp", scatter_dimension=0, tiled=False)

    def home(outputs):
        def add(wanted, group, received, shapes):
            flops = len(wanted) * pick_flops * (2 if outputs else 1)
            return call(
                part(fold, wanted, outputs, len(shapes)), "fold", shapes,
                (z, routes, back[group], *received), flops, True,
            )

        one, whole = of((half, width), BF), of((count, width), BF)
        low, high = add([(far, 0, [], [])], len(groups) - 1, [], [one, one])
        from_below, from_above = up(low), down(high)
        for k in range(far - 1, 0, -1):
            first = k == far - 1
            group = groups[k - 1]
            wanted = [
                (k, group.index(k), [(0, not first)], [] if first else [(0, True)]),
                (-k, group.index(-k), [] if first else [(1, True)], [(1, not first)]),
            ]
            right, left = add(wanted, k - 1, [from_below, from_above], [whole, whole])
            from_below, from_above = up(right), down(left)
        everything = [(0, True), (1, True)]
        return add([(0, 0, everything, everything)], 0, [from_below, from_above], [whole])[0]

    mixed = home(True)
    grad_tokens = home(False)
    ordered = jnp.stack([grads[o] for o in range(planes)] * 2)
    ordered = lax.dynamic_slice_in_dim(ordered, lax.rem(planes - z[0], planes), planes, 0)
    at_home = lax.all_to_all(ordered, "z", 0, 0, tiled=True).reshape(experts, count)
    grad_combine = call(by_choice, "by_choice", of((count, top), F32), (ids, at_home), 0)
    return (mixed, grad_tokens, grad_combine, summed[0][None], summed[1][None], summed[2].T[None])


def solution(mesh):
    devices = mesh.devices
    peers = 8
    split = Mesh(devices.reshape(devices.shape[0], -1, peers // 2, 2), ("dp", "z", "y", "core"))
    rows = P(("dp", "z", "y", "core"), None)
    expert = ("z", "y", "core")
    deep, wide = P(expert, "dp", None), P(expert, None, "dp")
    return jax.shard_map(
        on_device,
        mesh=split,
        in_specs=(rows, rows, rows, rows, P(), deep, deep, wide),
        out_specs=(rows, rows, rows, deep, deep, wide),
        check_vma=False,
    )
```

```python
import functools

import jax
import jax.numpy as jnp
from jax import lax
from jax.experimental import pallas as pl
from jax.experimental.pallas import tpu as pltpu
from jax.sharding import Mesh, PartitionSpec as P

SMALL_VMEM = 60 * 2**20
LARGE_VMEM = 60 * 2**20
BF = jnp.bfloat16
F32 = jnp.float32
STEP = 512
INFO = 16
SCALE = 1000


def together(*arrays):
    return lax.optimization_barrier(arrays)


def contract(left, right, left_dim, right_dim):
    return lax.dot_general(
        left, right, (((left_dim,), (right_dim,)), ((), ())), preferred_element_type=F32
    )


def call(body, name, out_shape, args, flops, scalar=False, scratch=()):
    outs = out_shape if isinstance(out_shape, (tuple, list)) else [out_shape]
    moved = sum(a.size * a.dtype.itemsize for a in (*args, *outs))
    specs = [pl.BlockSpec(memory_space=pltpu.VMEM) for _ in args]
    if scalar:
        specs[0] = pl.BlockSpec(memory_space=pltpu.SMEM)
    return pl.pallas_call(
        body,
        out_shape=out_shape,
        in_specs=specs,
        scratch_shapes=scratch,
        name=name,
        compiler_params=pltpu.CompilerParams(vmem_limit_bytes=LARGE_VMEM if name in ("expert_math", "weight_grads") else SMALL_VMEM),
        cost_estimate=pl.CostEstimate(flops=flops // SCALE, bytes_accessed=moved // SCALE, transcendentals=0),
    )(*args)


def split_three(x):
    high = x.astype(BF).astype(F32)
    mid = (x - high).astype(BF).astype(F32)
    return high, mid, x - high - mid


def route(experts, ids_ref, cap_ref, comb_ref, tokens_ref, out_ref):
    ids = ids_ref[...]
    comb = comb_ref[...]
    count, top = ids.shape
    lanes = lax.broadcasted_iota(jnp.int32, (count, 128), 1)
    chosen = jnp.zeros((count, 128), F32)
    weights = jnp.zeros((count, 128), F32)
    for k in range(top):
        hit = ids[:, k : k + 1] == lanes
        chosen = chosen + hit.astype(F32)
        weights = weights + jnp.where(hit, comb[:, k : k + 1], 0.0)
    earlier = (
        lax.broadcasted_iota(jnp.int32, (count, count), 1)
        < lax.broadcasted_iota(jnp.int32, (count, count), 0)
    ).astype(BF)
    rank = contract(earlier, chosen.astype(BF), 1, 0)
    kept = (chosen > 0.5) & (rank < cap_ref[...].astype(F32))
    parts = (jnp.where(kept, rank, -1.0).T, *split_three(weights.T))
    for j in range(experts // 4):
        block = jnp.concatenate([p[4 * j : 4 * j + 4] for p in parts], axis=0)
        out_ref[count:, 128 * j : 128 * j + 128] = block.astype(BF)
    out_ref[:count, :] = tokens_ref[...]


def stack_weights(gate_ref, up_ref, down_ref, out_ref):
    out_ref[0] = gate_ref[...]
    out_ref[1] = up_ref[...]
    out_ref[2] = down_ref[...].T


def slot_hits(info, peers, slots):
    count = info.shape[1]
    wanted = lax.broadcasted_iota(jnp.int32, (peers, slots, count), 1).astype(F32)
    held = (jnp.broadcast_to(info[:peers, None, :], (peers, slots, count)) == wanted).astype(F32)
    held = held.reshape(peers * slots, count)
    weight = jnp.broadcast_to(info[peers:, None, :], (peers, slots, count)).reshape(peers * slots, count)
    return held, held * weight


def columns(refs, c, count):
    if len(refs) == 1:
        return refs[0][:count, c : c + STEP]
    half = count // 2
    return jnp.concatenate([r[:half, c : c + STEP] for r in refs], axis=0)


def pick_rows(count, pieces, z_ref, *refs):
    out_ref, info_ref = refs[-2:]
    peers, n, slots, double = out_ref.shape
    width = double // 2
    lane = pl.multiple_of(z_ref[0] * 256, 256)
    for j in range(n):
        x_refs = refs[j * pieces : (j + 1) * pieces]
        g_refs = refs[(n + j) * pieces : (n + j + 1) * pieces]
        block = x_refs[-1][x_refs[-1].shape[0] - INFO :, pl.ds(lane, 256)].astype(F32)
        by_expert = [
            jnp.concatenate([block[r : r + 4, :128], block[r : r + 4, 128:]], axis=0) for r in range(0, INFO, 4)
        ]
        info = jnp.concatenate([by_expert[0], by_expert[1] + by_expert[2] + by_expert[3]], axis=0)
        info_ref[j] = info
        held, share = slot_hits(info, peers, slots)
        scale = jnp.sum(share, axis=1, keepdims=True)
        pick = held.astype(BF)
        for c in range(0, width, STEP):
            rows = contract(pick, columns(x_refs, c, count), 1, 0)
            out_ref[:, j, :, c : c + STEP] = rows.reshape(peers, slots, STEP).astype(BF)
            rows = scale * contract(pick, columns(g_refs, c, count), 1, 0)
            out_ref[:, j, :, width + c : width + c + STEP] = rows.reshape(peers, slots, STEP).astype(BF)


def expert_math(xg_ref, w_ref, od_ref, saved_ref):
    parts, _, deep, hidden = w_ref.shape
    width = parts * deep

    def over_width(start, which):
        return sum(
            contract(xg_ref[:, start + d * deep : start + (d + 1) * deep], w_ref[d, which], 1, 0)
            for d in range(parts)
        )

    h = over_width(0, 0)
    u = over_width(0, 1)
    s = jax.nn.sigmoid(h)
    a = (h * s * u).astype(BF)
    saved_ref[:, :hidden] = a
    for d in range(parts):
        od_ref[:, d * deep : (d + 1) * deep] = contract(a, w_ref[d, 2], 1, 1).astype(BF)
    da = over_width(width, 2)
    dh = (da * u * s * (1.0 + h * (1.0 - s))).astype(BF)
    du = (da * h * s).astype(BF)
    saved_ref[:, hidden : 2 * hidden] = dh
    saved_ref[:, 2 * hidden :] = du
    for d in range(parts):
        od_ref[:, width + d * deep : width + (d + 1) * deep] = (
            contract(dh, w_ref[d, 0], 1, 1) + contract(du, w_ref[d, 1], 1, 1)
        ).astype(BF)


def weight_grads(groups, *refs):
    xg, saved = refs[:groups], refs[groups : 2 * groups]
    out_ref = refs[-1]
    parts, _, deep, hidden = out_ref.shape
    width = parts * deep
    saved = jnp.concatenate([r[...] for r in saved], axis=0)
    a, dh, du = (saved[:, i * hidden : (i + 1) * hidden] for i in range(3))
    for d in range(parts):
        x = jnp.concatenate([r[:, d * deep : (d + 1) * deep] for r in xg], axis=0)
        out_ref[d, 0] = contract(x, dh, 0, 0).astype(BF)
        out_ref[d, 1] = contract(x, du, 0, 0).astype(BF)
        g = jnp.concatenate([r[:, width + d * deep : width + (d + 1) * deep] for r in xg], axis=0)
        out_ref[d, 2] = contract(g, a, 0, 0).astype(BF)


def slot_rows(back_ref, j, c):
    peers, _, slots, _ = back_ref.shape
    return back_ref[:, j, :, c : c + STEP].astype(F32).reshape(peers * slots, STEP).astype(BF)


def combine_grads(pieces, info_ref, back_ref, *refs):
    out_ref = refs[-1]
    peers, n, slots, double = back_ref.shape
    count = info_ref.shape[2]
    for j in range(n):
        g_refs = refs[j * pieces : (j + 1) * pieces]
        held, _ = slot_hits(info_ref[j], peers, slots)
        dots = jnp.zeros(held.shape, F32)
        for c in range(0, double // 2, STEP):
            dots = dots + contract(slot_rows(back_ref, j, c), columns(g_refs, c, count), 1, 1)
        out_ref[j] = jnp.sum((held * dots).reshape(peers, slots, count), axis=1)


def token_sums(outputs, info, back_ref, j):
    peers, _, slots, double = back_ref.shape
    held, share = slot_hits(info, peers, slots)
    high = (share if outputs else held).astype(BF)
    low = (share - high.astype(F32)).astype(BF)

    def at(c):
        rows = slot_rows(back_ref, j, c + (0 if outputs else double // 2))
        total = contract(high, rows, 0, 0)
        return total + contract(low, rows, 0, 0) if outputs else total

    return at


def grads_block(grads):
    parts = split_three(grads)
    sides = [
        jnp.concatenate([*(p[i : i + 4] for p in parts), jnp.zeros((4, 128), F32)], axis=0) for i in (0, 4)
    ]
    return jnp.concatenate(sides, axis=1).astype(BF)


def fold_first(outputs, z_ref, info_ref, back_ref, grads_ref, low_ref, high_ref):
    half = info_ref.shape[2] // 2
    width = low_ref.shape[1]
    total = token_sums(outputs, info_ref[0], back_ref, 0)
    for c in range(0, width, STEP):
        sums = total(c)
        low_ref[:, c : c + STEP] = sums[:half].astype(BF)
        high_ref[:half, c : c + STEP] = sums[half:].astype(BF)
    if outputs:
        high_ref[half:, :] = jnp.zeros((INFO, width), BF)
        high_ref[half:, pl.ds(pl.multiple_of(z_ref[0] * 256, 256), 256)] = grads_block(grads_ref[0])


def fold(outputs, halves, z_ref, info_ref, back_ref, grads_ref, below_ref, above_ref, right_ref, left_ref):
    count = info_ref.shape[2]
    half = count // 2
    width = right_ref.shape[1]
    for out_ref, in_ref, j in ((right_ref, below_ref, 1), (left_ref, above_ref, 0)):
        j = j + info_ref.shape[0] - 2
        total = token_sums(outputs, info_ref[j], back_ref, j)
        for c in range(0, width, STEP):
            sums = total(c)
            if not halves:
                out_ref[:count, c : c + STEP] = (sums + in_ref[:count, c : c + STEP].astype(F32)).astype(BF)
                continue
            low, high = sums[:half], sums[half:]
            if out_ref is right_ref:
                low = low + in_ref[:half, c : c + STEP].astype(F32)
            else:
                high = high + in_ref[:half, c : c + STEP].astype(F32)
            out_ref[:half, c : c + STEP] = low.astype(BF)
            out_ref[half:count, c : c + STEP] = high.astype(BF)
        if outputs:
            if halves and out_ref is right_ref:
                out_ref[count:, :] = jnp.zeros((INFO, width), BF)
            else:
                out_ref[count:, :] = in_ref[in_ref.shape[0] - INFO :, :]
            lane = pl.multiple_of(z_ref[0] * 256, 256)
            out_ref[count:, pl.ds(lane, 256)] = grads_block(grads_ref[j])


def fold_last(outputs, z_ref, ids_ref, info_ref, back_ref, grads_ref, below_ref, above_ref, out_ref, gc_ref, held_ref):
    count = info_ref.shape[2]
    width = out_ref.shape[1]
    total = token_sums(outputs, info_ref[0], back_ref, 0)
    for c in range(0, width, STEP):
        arrived = below_ref[:count, c : c + STEP].astype(F32) + above_ref[:count, c : c + STEP].astype(F32)
        out_ref[:, c : c + STEP] = (total(c) + arrived).astype(BF)
    if not outputs:
        return
    held_ref[...] = below_ref[count:, :].astype(F32) + above_ref[count:, :].astype(F32)
    held_ref[:, pl.ds(pl.multiple_of(z_ref[0] * 256, 256), 256)] = grads_block(grads_ref[0]).astype(F32)
    rows = []
    for c in range(0, width, 128):
        block = held_ref[:, c : c + 128]
        rows.append(block[0:4] + block[4:8] + block[8:12])
    pad = jnp.zeros((128 - 4 * len(rows), count), F32)
    by_token = jnp.concatenate([*rows, pad] if pad.shape[0] else rows, axis=0).T
    ids = ids_ref[...]
    lanes = lax.broadcasted_iota(jnp.int32, (count, 128), 1)
    for k in range(ids.shape[1]):
        gc_ref[:, k : k + 1] = jnp.sum(
            jnp.where(ids[:, k : k + 1] == lanes, by_token, 0.0), axis=1, keepdims=True
        )


def on_device(tokens, cotangent, ids, combine, capacity, w_gate, w_up, w_down):
    part = functools.partial
    of = jax.ShapeDtypeStruct
    planes = lax.axis_size("z")
    peers = lax.axis_size("y") * lax.axis_size("core")
    count, width = tokens.shape
    top = ids.shape[1]
    experts = capacity.shape[0]
    slots = count * top // (2 * experts)
    hidden = w_gate.shape[2]
    half = count // 2
    far = planes // 2
    limits = jnp.pad(capacity, (0, 128 - experts)).reshape(1, 128)
    z = lax.axis_index("z").astype(jnp.int32).reshape(1)

    def up(x):
        return lax.ppermute(x, "z", [(i, (i + 1) % planes) for i in range(planes)])

    def down(x):
        return lax.ppermute(x, "z", [(i, (i - 1) % planes) for i in range(planes)])

    def across(x):
        return lax.all_to_all(x, ("y", "core"), 0, 0, tiled=True)

    table = call(
        part(route, experts), "route", of((count + INFO, width), BF), (ids, limits, combine, tokens),
        2 * count * count * 128,
    )
    unit = 2 * peers * slots * width * hidden
    pick_flops = 2 * peers * slots * count * width

    def fill(xs, gs):
        n = len(xs)
        return call(
            part(pick_rows, count, len(xs[0])), "pick_rows",
            [of((peers, n, slots, 2 * width), BF), of((n, 2 * peers, count), F32)],
            (z, *sum(xs, []), *sum(gs, [])), 2 * n * pick_flops, True,
        )

    def swap(sent):
        return across(sent).reshape(-1, 2 * width)

    def work(xg):
        rows = xg.shape[0]
        return call(
            expert_math, "expert_math",
            [of((rows, 2 * width), BF), of((rows, 3 * hidden), BF)],
            (xg, weights), 6 * rows * unit // (peers * slots),
        )

    def back_home(od, info, gs):
        n = info.shape[0]
        back = across(od.reshape(peers, n, slots, 2 * width))
        grads = call(
            part(combine_grads, len(gs[0])), "combine_grads", of((n, peers, count), F32),
            (info, back, *sum(gs, [])), n * pick_flops,
        )
        return back, grads

    stacked = call(
        stack_weights, "stack_weights", of((3, *w_gate.shape[1:]), BF), (w_gate[0], w_up[0], w_down[0]), 0
    )
    weights = lax.all_gather(stacked, "dp", axis=0, tiled=False)
    first, _ = together(cotangent, stacked)
    g_up, g_down = up(first), down(first)
    x_up, x_down = up(table), down(table)
    xs, gs = [[table], [x_up], [x_down]], [[cotangent], [g_up], [g_down]]
    xgs, infos, g_rows = [], [], []
    sent = None
    for step in range(2, far):
        g_up, g_down = up(g_up), down(g_down)
        x_up, x_down = up(x_up), down(x_down)
        if sent is not None:
            xgs.append(swap(sent))
        sent, info = fill(xs, gs)
        infos.append(info)
        g_rows.append(gs)
        xs, gs = [[x_up], [x_down]], [[g_up], [g_down]]
        g_up, g_down, sent = together(g_up, g_down, sent)
    g_low, g_high = up(g_up[:half]), down(g_down[half:])
    xgs.append(swap(sent))
    x_up, x_down, xgs[0] = together(x_up, x_down, xgs[0])
    x_low, x_high = up(x_up[:half]), down(x_down[half:])
    sent, info = fill(xs, gs)
    infos.append(info)
    g_rows.append(gs)
    xgs.append(swap(sent))
    done = [work(xg) for xg in xgs[:-1]]
    x_low, x_high, *_ = together(x_low, x_high, xgs[-2], *(d[0] for d in done))
    xs, gs = [[x_low, x_high]], [[g_low, g_high]]
    sent, info = fill(xs, gs)
    infos.append(info)
    g_rows.append(gs)
    sent, xgs[-1] = together(sent, xgs[-1])
    xg = swap(sent)
    done.append(work(xgs[-1]))
    xg, _ = together(xg, done[-1][0])
    xgs.append(xg)
    done.append(work(xg))
    od = [d[0] for d in done]

    tall, whole = of((count + INFO, width), BF), of((count, width), BF)
    last = len(xgs) - 1
    back, grads = back_home(od[last], infos[last], g_rows[last])
    args = (z, infos[last], back, grads)
    o_low, o_high = call(
        part(fold_first, True), "fold_first", [of((half, width), BF), of((half + INFO, width), BF)], args, 2 * pick_flops, True
    )
    late, _ = together(od[last - 1], o_low)
    held, _ = together(back, o_low)
    args = (z, infos[last], held, grads)
    d_low, d_high = call(part(fold_first, False), "fold_first", [of((half, width), BF)] * 2, args, pick_flops, True)
    o_below, o_above, d_below, d_above = up(o_low), down(o_high), up(d_low), down(d_high)
    first, before = (o_below, o_above, d_below, d_above), d_low
    for k in range(last - 1, -1, -1):
        back, grads = back_home(late, infos[k], g_rows[k])
        args = (z, infos[k], back, grads)
        halves = k == last - 1
        if halves:
            o_below, o_above, d_below, d_above = together(o_below, o_above, d_below, d_above)
        o_below, o_above, _ = together(o_below, o_above, before)
        o_right, o_left = call(
            part(fold, True, halves), "fold", [tall, tall], (*args, o_below, o_above), 4 * pick_flops, True
        )
        if k:
            late, _ = together(od[k - 1], o_right)
        d_below, d_above, _ = together(d_below, d_above, o_right)
        d_right, d_left = call(
            part(fold, False, halves), "fold", [whole, whole], (*args, d_below, d_above), 2 * pick_flops, True
        )
        before = d_right
        if halves:
            saved = [d[1] for d in done]
            saved[0], *_ = together(saved[0], *first)
            partial_grads = call(
                part(weight_grads, len(xgs)), "weight_grads", of(weights.shape, BF),
                (*xgs, *saved), 3 * planes * unit,
            )
            summed = lax.psum_scatter(partial_grads, "dp", scatter_dimension=0, tiled=False)
        o_below, o_above, d_below, d_above = up(o_right), down(o_left), up(d_right), down(d_left)
    grad_down = summed[2].T
    d_below, d_above, grad_down = together(d_below, d_above, grad_down)
    small = pltpu.VMEM((INFO, width), F32)
    args = (z, ids, infos[0], back, grads)
    mixed, grad_combine = call(
        part(fold_last, True), "fold_last", [whole, of((count, top), F32)], (*args, o_below, o_above), 2 * pick_flops, True, [small]
    )
    grad_tokens, _ = call(
        part(fold_last, False), "fold_last", [whole, of((count, top), F32)], (*args, d_below, d_above), pick_flops, True, [small]
    )
    return (mixed, grad_tokens, grad_combine, summed[0][None], summed[1][None], grad_down[None])


def solution(mesh):
    devices = mesh.devices
    peers = 8
    split = Mesh(devices.reshape(devices.shape[0], -1, peers // 2, 2), ("dp", "z", "y", "core"))
    rows = P(("dp", "z", "y", "core"), None)
    expert = ("z", "y", "core")
    deep, wide = P(expert, "dp", None), P(expert, None, "dp")
    return jax.shard_map(
        on_device,
        mesh=split,
        in_specs=(rows, rows, rows, rows, P(), deep, deep, wide),
        out_specs=(rows, rows, rows, deep, deep, wide),
        check_vma=False,
    )
```

```python
import functools

import jax
import jax.numpy as jnp
from jax import lax
from jax.experimental import pallas as pl
from jax.experimental.pallas import tpu as pltpu
from jax.sharding import PartitionSpec as P

MIB = 2**20
BF = jnp.bfloat16
F32 = jnp.float32
STEP = 512


def contract(left, right, left_dim, right_dim):
    return lax.dot_general(
        left, right, (((left_dim,), (right_dim,)), ((), ())), preferred_element_type=F32
    )


def together(*arrays):
    return lax.optimization_barrier(arrays)


def hits(ids_ref, cap_ref, slots):
    top, count = ids_ref.shape
    experts = cap_ref.shape[1]
    numbers = lax.broadcasted_iota(jnp.int32, (experts, count), 0)
    chosen = [ids_ref[k : k + 1, :] == numbers for k in range(top)]
    taken = sum(c.astype(F32) for c in chosen)
    earlier = (
        lax.broadcasted_iota(jnp.int32, (count, count), 0)
        < lax.broadcasted_iota(jnp.int32, (count, count), 1)
    ).astype(BF)
    rank = contract(taken.astype(BF), earlier, 1, 0)
    same = lax.broadcasted_iota(jnp.int32, (experts, experts), 0) == lax.broadcasted_iota(
        jnp.int32, (experts, experts), 1
    )
    limit = jnp.sum(jnp.where(same, cap_ref[...].astype(F32), 0.0), axis=1, keepdims=True)
    slot_of = jnp.where((taken > 0.5) & (rank < limit), rank, -1.0)
    wanted = lax.broadcasted_iota(jnp.int32, (experts, slots, count), 1).astype(F32)
    held = (jnp.broadcast_to(slot_of[:, None, :], (experts, slots, count)) == wanted).astype(F32)
    return held.reshape(experts * slots, count), chosen


def shares(held, chosen, comb_ref, slots):
    weights = sum(jnp.where(c, comb_ref[k : k + 1, :], 0.0) for k, c in enumerate(chosen))
    experts, count = weights.shape
    spread = jnp.broadcast_to(weights[:, None, :], (experts, slots, count)).reshape(experts * slots, count)
    return held * spread


def pick_rows(slots, ids_ref, cap_ref, comb_ref, tokens_ref, cot_ref, out_ref, pick_ref, scale_ref):
    i = pl.program_id(0)
    steps = pl.num_programs(0)

    @pl.when(i == 0)
    def _():
        held, chosen = hits(ids_ref, cap_ref, slots)
        pick_ref[...] = held.astype(BF)
        scale = jnp.sum(shares(held, chosen, comb_ref, slots), axis=1, keepdims=True)
        scale_ref[...] = jnp.broadcast_to(scale, scale_ref.shape)

    wide = out_ref.shape[1]

    @pl.when(i < steps // 2)
    def _():
        for c in range(0, wide, STEP):
            out_ref[:, c : c + STEP] = contract(pick_ref[...], tokens_ref[:, c : c + STEP], 1, 0).astype(BF)

    @pl.when(i >= steps // 2)
    def _():
        scale = scale_ref[:, :1]
        for c in range(0, wide, STEP):
            rows = contract(pick_ref[...], cot_ref[:, c : c + STEP], 1, 0)
            out_ref[:, c : c + STEP] = (scale * rows).astype(BF)


def stack_weights(gate_ref, up_ref, down_ref, out_ref):
    out_ref[0] = gate_ref[...]
    out_ref[1] = up_ref[...]
    out_ref[2] = down_ref[...].T


def expert_math(xg_hbm, w_hbm, od_hbm, saved_ref, xg_ref, w_ref, od_ref, in_sems, w_sems, out_sems):
    parts, _, deep, hidden = w_ref.shape

    def piece(ref, d):
        return ref.at[:, pl.ds(d * deep, deep)]

    def arrive(d):
        return pltpu.make_async_copy(piece(xg_hbm, d), piece(xg_ref, d), in_sems.at[d])

    def weights(d):
        if d < parts:
            return pltpu.make_async_copy(w_hbm.at[d, pl.ds(0, 2)], w_ref.at[d, pl.ds(0, 2)], w_sems.at[d])
        d -= parts
        return pltpu.make_async_copy(w_hbm.at[d, 2], w_ref.at[d, 2], w_sems.at[parts + d])

    def leave(d):
        return pltpu.make_async_copy(piece(od_ref, d), piece(od_hbm, d), out_sems.at[d])

    for d in range(parts):
        weights(d).start()
        arrive(d).start()
    for d in range(parts):
        weights(parts + d).start()
    for d in range(parts):
        arrive(parts + d).start()
    h = u = da = 0.0
    for d in range(parts):
        weights(d).wait()
        arrive(d).wait()
        x = xg_ref[:, d * deep : (d + 1) * deep]
        h = h + contract(x, w_ref[d, 0], 1, 0)
        u = u + contract(x, w_ref[d, 1], 1, 0)
    s = jax.nn.sigmoid(h)
    a = (h * s * u).astype(BF)
    saved_ref[:, :hidden] = a
    for d in range(parts):
        weights(parts + d).wait()
        od_ref[:, d * deep : (d + 1) * deep] = contract(a, w_ref[d, 2], 1, 1).astype(BF)
        leave(d).start()
    for d in range(parts):
        arrive(parts + d).wait()
        da = da + contract(xg_ref[:, (parts + d) * deep : (parts + d + 1) * deep], w_ref[d, 2], 1, 0)
    dh = (da * u * s * (1.0 + h * (1.0 - s))).astype(BF)
    du = (da * h * s).astype(BF)
    saved_ref[:, hidden : 2 * hidden] = dh
    saved_ref[:, 2 * hidden :] = du
    for d in range(parts):
        n = parts + d
        od_ref[:, n * deep : (n + 1) * deep] = (
            contract(dh, w_ref[d, 0], 1, 1) + contract(du, w_ref[d, 1], 1, 1)
        ).astype(BF)
        leave(n).start()
    for d in range(2 * parts):
        leave(d).wait()


def unstack_weights(in_ref, gate_ref, up_ref, down_ref):
    gate_ref[...] = in_ref[0]
    up_ref[...] = in_ref[1]
    down_ref[...] = in_ref[2].T


def weight_grads(x_ref, g_ref, saved_ref, out_ref):
    hidden = out_ref.shape[3]
    a, dh, du = (saved_ref[:, i * hidden : (i + 1) * hidden] for i in range(3))
    x = x_ref[...]
    out_ref[0, 0] = contract(x, dh, 0, 0).astype(BF)
    out_ref[0, 1] = contract(x, du, 0, 0).astype(BF)
    out_ref[0, 2] = contract(g_ref[...], a, 0, 0).astype(BF)


def merge(
    slots, ids_ref, cap_ref, comb_ref, cot_ref, o_ref, d_ref, mixed_ref, rows_ref, gc_ref, high_ref, low_ref, pick_ref, dots_ref
):
    i = pl.program_id(0)

    @pl.when(i == 0)
    def _():
        held, chosen = hits(ids_ref, cap_ref, slots)
        share = shares(held, chosen, comb_ref, slots)
        high = share.astype(BF)
        pick_ref[...] = held.astype(BF)
        high_ref[...] = high
        low_ref[...] = (share - high.astype(F32)).astype(BF)
        dots_ref[...] = jnp.zeros(dots_ref.shape, F32)

    o = o_ref[...]
    mixed_ref[...] = (contract(high_ref[...], o, 0, 0) + contract(low_ref[...], o, 0, 0)).astype(BF)
    rows_ref[...] = contract(pick_ref[...], d_ref[...], 0, 0).astype(BF)
    dots_ref[...] += contract(o, cot_ref[...], 1, 1)

    @pl.when(i == pl.num_programs(0) - 1)
    def _():
        top, count = ids_ref.shape
        experts = cap_ref.shape[1]
        found = dots_ref[...] * pick_ref[...].astype(F32)
        per_expert = jnp.sum(found.reshape(experts, slots, count), axis=1)
        numbers = lax.broadcasted_iota(jnp.int32, (experts, count), 0)
        for k in range(top):
            hit = ids_ref[k : k + 1, :] == numbers
            gc_ref[k : k + 1, :] = jnp.sum(jnp.where(hit, per_expert, 0.0), axis=0, keepdims=True)


def on_device(tokens, cotangent, expert_ids, combine, capacity, w_gate, w_up, w_down):
    part = functools.partial
    of = jax.ShapeDtypeStruct
    peers = lax.axis_size("expert")
    count, width = tokens.shape
    top = expert_ids.shape[1]
    experts = capacity.shape[0]
    slots = count * top // (2 * peers)
    rows = experts * slots
    hidden = w_gate.shape[2]
    limits = capacity.reshape(1, experts)
    ids, comb = expert_ids.T, combine.T
    unit = 2 * rows * width * hidden
    pick_flops = 2 * rows * count * width

    def cost(flops, moved):
        return pl.CostEstimate(flops=flops, bytes_accessed=moved, transcendentals=0)

    def room(mib):
        return pltpu.CompilerParams(vmem_limit_bytes=mib * MIB)

    def fixed(shape):
        return pl.BlockSpec(shape, lambda i: (0,) * len(shape))

    def exchange(x):
        x = x.reshape(peers, slots, 2 * width)
        return lax.all_to_all(x, "expert", 0, 0, tiled=True).reshape(rows, 2 * width)

    block = width // 2
    sent = pl.pallas_call(
        part(pick_rows, slots),
        grid=(4,),
        in_specs=[
            fixed((top, count)), fixed((1, experts)), fixed((top, count)),
            pl.BlockSpec((count, block), lambda i: (0, jnp.minimum(i, 1))),
            pl.BlockSpec((count, block), lambda i: (0, jnp.maximum(i - 2, 0))),
        ],
        out_specs=pl.BlockSpec((rows, block), lambda i: (0, i)),
        out_shape=of((rows, 2 * width), BF),
        scratch_shapes=[pltpu.VMEM((rows, count), BF), pltpu.VMEM((rows, 128), F32)],
        name="pick_rows", compiler_params=room(60), cost_estimate=cost(2 * pick_flops, 5 * rows * width),
    )(ids, limits, comb, tokens, cotangent)
    xg = exchange(sent)

    parts = lax.axis_size("dp")
    deep = width // parts
    stacked = pl.pallas_call(
        stack_weights, out_shape=of((3, deep, hidden), BF), name="stack_weights", compiler_params=room(16),
        cost_estimate=cost(0, 12 * deep * hidden),
    )(w_gate[0], w_up[0], w_down[0])
    weights = lax.all_gather(stacked, "dp", axis=0, tiled=False)

    whole = pl.BlockSpec(memory_space=pl.ANY)
    od, saved = pl.pallas_call(
        expert_math,
        in_specs=[whole, whole],
        out_specs=[whole, pl.BlockSpec(memory_space=pltpu.VMEM)],
        out_shape=[of((rows, 2 * width), BF), of((rows, 3 * hidden), BF)],
        scratch_shapes=[
            pltpu.VMEM((rows, 2 * width), BF), pltpu.VMEM(weights.shape, BF), pltpu.VMEM((rows, 2 * width), BF),
            pltpu.SemaphoreType.DMA((2 * parts,)), pltpu.SemaphoreType.DMA((2 * parts,)), pltpu.SemaphoreType.DMA((2 * parts,)),
        ],
        name="expert_math", compiler_params=room(60), cost_estimate=cost(6 * unit, 10 * rows * width),
    )(xg, weights)
    back = exchange(od)

    partial_grads = pl.pallas_call(
        weight_grads,
        grid=(parts,),
        in_specs=[
            pl.BlockSpec((rows, deep), lambda d: (0, d)),
            pl.BlockSpec((rows, deep), lambda d: (0, d + width // deep)),
            fixed((rows, 3 * hidden)),
        ],
        out_specs=pl.BlockSpec((1, 3, deep, hidden), lambda d: (d, 0, 0, 0)),
        out_shape=of((parts, 3, deep, hidden), BF),
        name="weight_grads", compiler_params=room(60), cost_estimate=cost(3 * unit, 6 * rows * width),
    )(xg, xg, saved)
    summed = lax.psum_scatter(partial_grads, "dp", scatter_dimension=0, tiled=False)
    grad_gate, grad_up, grad_down = pl.pallas_call(
        unstack_weights, out_shape=[of((deep, hidden), BF), of((deep, hidden), BF), of((hidden, deep), BF)],
        name="unstack_weights", compiler_params=room(16), cost_estimate=cost(0, 12 * deep * hidden),
    )(summed)
    back, grad_gate, grad_up, grad_down = together(back, grad_gate, grad_up, grad_down)

    mixed, grad_tokens, grad_combine = pl.pallas_call(
        part(merge, slots),
        grid=(width // STEP,),
        in_specs=[
            fixed((top, count)), fixed((1, experts)), fixed((top, count)),
            pl.BlockSpec((count, STEP), lambda i: (0, i)),
            pl.BlockSpec((rows, STEP), lambda i: (0, i)),
            pl.BlockSpec((rows, STEP), lambda i: (0, i + width // STEP)),
        ],
        out_specs=[
            pl.BlockSpec((count, STEP), lambda i: (0, i)), pl.BlockSpec((count, STEP), lambda i: (0, i)), fixed((top, count)),
        ],
        out_shape=[of((count, width), BF), of((count, width), BF), of((top, count), F32)],
        scratch_shapes=[pltpu.VMEM((rows, count), BF)] * 3 + [pltpu.VMEM((rows, count), F32)],
        name="merge", compiler_params=room(60), cost_estimate=cost(4 * pick_flops, 5 * rows * width),
    )(ids, limits, comb, cotangent, back, back)
    return (mixed, grad_tokens, grad_combine.T, grad_gate[None], grad_up[None], grad_down[None])


def solution(mesh):
    rows = P(("dp", "expert"), None)
    deep, wide = P("expert", "dp", None), P("expert", None, "dp")
    return jax.shard_map(
        on_device,
        mesh=mesh,
        in_specs=(rows, rows, rows, rows, P(), deep, deep, wide),
        out_specs=(rows, rows, rows, deep, deep, wide),
        check_vma=False,
    )
```

```python
import functools

import jax
import jax.numpy as jnp
from jax import lax
from jax.experimental import pallas as pl
from jax.experimental.pallas import tpu as pltpu
from jax.sharding import PartitionSpec as P

MIB = 2**20
BF = jnp.bfloat16
F32 = jnp.float32
STEP = 512


def contract(left, right, left_dim, right_dim):
    return lax.dot_general(
        left, right, (((left_dim,), (right_dim,)), ((), ())), preferred_element_type=F32
    )


def together(*arrays):
    return lax.optimization_barrier(arrays)


def hits(ids_ref, cap_ref, slots):
    top, count = ids_ref.shape
    experts = cap_ref.shape[1]
    numbers = lax.broadcasted_iota(jnp.int32, (experts, count), 0)
    chosen = [ids_ref[k : k + 1, :] == numbers for k in range(top)]
    taken = sum(c.astype(F32) for c in chosen)
    earlier = (
        lax.broadcasted_iota(jnp.int32, (count, count), 0)
        < lax.broadcasted_iota(jnp.int32, (count, count), 1)
    ).astype(BF)
    rank = contract(taken.astype(BF), earlier, 1, 0)
    same = lax.broadcasted_iota(jnp.int32, (experts, experts), 0) == lax.broadcasted_iota(
        jnp.int32, (experts, experts), 1
    )
    limit = jnp.sum(jnp.where(same, cap_ref[...].astype(F32), 0.0), axis=1, keepdims=True)
    slot_of = jnp.where((taken > 0.5) & (rank < limit), rank, -1.0)
    wanted = lax.broadcasted_iota(jnp.int32, (experts, slots, count), 1).astype(F32)
    held = (jnp.broadcast_to(slot_of[:, None, :], (experts, slots, count)) == wanted).astype(F32)
    return held.reshape(experts * slots, count), chosen


def shares(held, chosen, comb_ref, slots):
    weights = sum(jnp.where(c, comb_ref[k : k + 1, :], 0.0) for k, c in enumerate(chosen))
    experts, count = weights.shape
    spread = jnp.broadcast_to(weights[:, None, :], (experts, slots, count)).reshape(experts * slots, count)
    return held * spread


def pick_rows(slots, ids_ref, cap_ref, comb_ref, tokens_ref, cot_ref, out_ref, pick_ref, high_ref, low_ref, scale_ref):
    i = pl.program_id(0)
    steps = pl.num_programs(0)

    @pl.when(i == 0)
    def _():
        held, chosen = hits(ids_ref, cap_ref, slots)
        pick_ref[...] = held.astype(BF)
        share = shares(held, chosen, comb_ref, slots)
        high_ref[...] = share.astype(BF)
        low_ref[...] = (share - share.astype(BF).astype(F32)).astype(BF)
        scale = jnp.sum(share, axis=1, keepdims=True)
        scale_ref[...] = jnp.broadcast_to(scale, scale_ref.shape)

    wide = out_ref.shape[1]

    @pl.when(i < steps // 2)
    def _():
        for c in range(0, wide, STEP):
            out_ref[:, c : c + STEP] = contract(pick_ref[...], tokens_ref[:, c : c + STEP], 1, 0).astype(BF)

    @pl.when(i >= steps // 2)
    def _():
        scale = scale_ref[:, :1]
        for c in range(0, wide, STEP):
            rows = contract(pick_ref[...], cot_ref[:, c : c + STEP], 1, 0)
            out_ref[:, c : c + STEP] = (scale * rows).astype(BF)


def lay_weights(gate_ref, up_ref, down_ref, out_ref):
    hidden = gate_ref.shape[1]
    out_ref[:, :hidden] = gate_ref[...]
    out_ref[:, hidden : 2 * hidden] = up_ref[...]
    out_ref[:, 2 * hidden :] = down_ref[...].T


def expert_math(
    me_ref, xg_hbm, own_hbm, next_hbm, far_low_hbm, far_high_hbm, prev_hbm, od_hbm, saved_ref, xg_ref, w_ref, od_ref, in_sems, w_sems, out_sems
):
    parts, deep, hidden = w_ref.shape
    hidden //= 3
    half = deep // 2
    order = (0, 1, 3, 2)

    def lanes(n):
        block = lax.rem(me_ref[0] + n % parts, parts) + n // parts * parts
        return pl.ds(pl.multiple_of(block * deep, deep), deep)

    def arrive(n):
        return pltpu.make_async_copy(xg_hbm.at[:, lanes(n)], xg_ref.at[:, pl.ds(n * deep, deep)], in_sems.at[n])

    def leave(n):
        return pltpu.make_async_copy(od_ref.at[:, pl.ds(n * deep, deep)], od_hbm.at[:, lanes(n)], out_sems.at[n])

    def weights(n):
        if n != 2:
            source = {0: own_hbm, 1: next_hbm, 3: prev_hbm}[n]
            return [pltpu.make_async_copy(source, w_ref.at[n], w_sems.at[n])]
        return [
            pltpu.make_async_copy(far_low_hbm, w_ref.at[n, pl.ds(0, half)], w_sems.at[n]),
            pltpu.make_async_copy(far_high_hbm, w_ref.at[n, pl.ds(half, half)], w_sems.at[parts]),
        ]

    for n in order:
        for copy in weights(n):
            copy.start()
        arrive(n).start()
    for n in order:
        arrive(parts + n).start()
    hu = da = 0.0
    for n in order:
        for copy in weights(n):
            copy.wait()
        arrive(n).wait()
        hu = hu + contract(xg_ref[:, n * deep : (n + 1) * deep], w_ref[n, :, : 2 * hidden], 1, 0)
    h, u = hu[:, :hidden], hu[:, hidden:]
    s = jax.nn.sigmoid(h)
    a = (h * s * u).astype(BF)
    saved_ref[:, 2 * hidden :] = a
    for n in order:
        od_ref[:, n * deep : (n + 1) * deep] = contract(a, w_ref[n, :, 2 * hidden :], 1, 1).astype(BF)
        leave(n).start()
    for n in order:
        arrive(parts + n).wait()
        g = xg_ref[:, (parts + n) * deep : (parts + n + 1) * deep]
        da = da + contract(g, w_ref[n, :, 2 * hidden :], 1, 0)
    dh = (da * u * s * (1.0 + h * (1.0 - s))).astype(BF)
    du = (da * h * s).astype(BF)
    saved_ref[:, :hidden] = dh
    saved_ref[:, hidden : 2 * hidden] = du
    both = jnp.concatenate([dh, du], axis=1)
    for n in order:
        m = parts + n
        od_ref[:, m * deep : (m + 1) * deep] = contract(both, w_ref[n, :, : 2 * hidden], 1, 1).astype(BF)
        leave(m).start()
    for n in range(2 * parts):
        leave(n).wait()


def weight_grads(me_ref, x_ref, g_ref, saved_ref, out_ref):
    hidden = out_ref.shape[2] // 3
    out_ref[0, :, : 2 * hidden] = contract(x_ref[...], saved_ref[:, : 2 * hidden], 0, 0).astype(BF)
    out_ref[0, :, 2 * hidden :] = contract(g_ref[...], saved_ref[:, 2 * hidden :], 0, 0).astype(BF)


def add_far(next_ref, prev_ref, low_ref, high_ref, right_ref, left_ref):
    half = low_ref.shape[0]
    right_ref[:half, :] = (next_ref[0, :half, :].astype(F32) + low_ref[...].astype(F32)).astype(BF)
    right_ref[half:, :] = next_ref[0, half:, :]
    left_ref[:half, :] = prev_ref[0, :half, :]
    left_ref[half:, :] = (prev_ref[0, half:, :].astype(F32) + high_ref[...].astype(F32)).astype(BF)


def add_last(own_ref, below_ref, above_ref, gate_ref, up_ref, down_ref):
    hidden = gate_ref.shape[1]
    total = own_ref[0].astype(F32) + below_ref[...].astype(F32) + above_ref[...].astype(F32)
    gate_ref[...] = total[:, :hidden].astype(BF)
    up_ref[...] = total[:, hidden : 2 * hidden].astype(BF)
    down_ref[...] = total[:, 2 * hidden :].astype(BF).T


def merge(
    slots, experts, ids_ref, pick_ref, high_ref, low_ref, cot_ref, o_ref, d_ref, mixed_ref, rows_ref, gc_ref, dots_ref
):
    i = pl.program_id(0)

    @pl.when(i == 0)
    def _():
        dots_ref[...] = jnp.zeros(dots_ref.shape, F32)

    o = o_ref[...]
    mixed_ref[...] = (contract(high_ref[...], o, 0, 0) + contract(low_ref[...], o, 0, 0)).astype(BF)
    rows_ref[...] = contract(pick_ref[...], d_ref[...], 0, 0).astype(BF)
    dots_ref[...] += contract(o, cot_ref[...], 1, 1)

    @pl.when(i == pl.num_programs(0) - 1)
    def _():
        top, count = ids_ref.shape
        found = dots_ref[...] * pick_ref[...].astype(F32)
        per_expert = jnp.sum(found.reshape(experts, slots, count), axis=1)
        numbers = lax.broadcasted_iota(jnp.int32, (experts, count), 0)
        for k in range(top):
            hit = ids_ref[k : k + 1, :] == numbers
            gc_ref[k : k + 1, :] = jnp.sum(jnp.where(hit, per_expert, 0.0), axis=0, keepdims=True)


def on_device(tokens, cotangent, expert_ids, combine, capacity, w_gate, w_up, w_down):
    part = functools.partial
    of = jax.ShapeDtypeStruct
    peers = lax.axis_size("expert")
    count, width = tokens.shape
    top = expert_ids.shape[1]
    experts = capacity.shape[0]
    slots = count * top // (2 * peers)
    rows = experts * slots
    hidden = w_gate.shape[2]
    limits = capacity.reshape(1, experts)
    ids, comb = expert_ids.T, combine.T
    unit = 2 * rows * width * hidden
    pick_flops = 2 * rows * count * width

    def cost(flops, moved):
        return pl.CostEstimate(flops=flops, bytes_accessed=moved, transcendentals=0)

    def room(mib):
        return pltpu.CompilerParams(vmem_limit_bytes=mib * MIB)

    def fixed(shape):
        return pl.BlockSpec(shape, lambda i: (0,) * len(shape))

    def exchange(x):
        x = x.reshape(peers, slots, 2 * width)
        return lax.all_to_all(x, "expert", 0, 0, tiled=True).reshape(rows, 2 * width)

    block = width // 2
    sent, *tables = pl.pallas_call(
        part(pick_rows, slots),
        grid=(4,),
        in_specs=[
            fixed((top, count)), fixed((1, experts)), fixed((top, count)),
            pl.BlockSpec((count, block), lambda i: (0, jnp.minimum(i, 1))),
            pl.BlockSpec((count, block), lambda i: (0, jnp.maximum(i - 2, 0))),
        ],
        out_specs=[pl.BlockSpec((rows, block), lambda i: (0, i))] + [fixed((rows, count))] * 3,
        out_shape=[of((rows, 2 * width), BF)] + [of((rows, count), BF)] * 3,
        scratch_shapes=[pltpu.VMEM((rows, 128), F32)],
        name="pick_rows", compiler_params=room(60), cost_estimate=cost(2 * pick_flops, 5 * rows * width),
    )(ids, limits, comb, tokens, cotangent)
    xg = exchange(sent)

    parts = lax.axis_size("dp")
    deep = width // parts
    half = deep // 2
    me = lax.axis_index("dp").astype(jnp.int32).reshape(1)

    def up(x):
        return lax.ppermute(x, "dp", [(i, (i + 1) % parts) for i in range(parts)])

    def down(x):
        return lax.ppermute(x, "dp", [(i, (i - 1) % parts) for i in range(parts)])

    own = pl.pallas_call(
        lay_weights, out_shape=of((deep, 3 * hidden), BF), name="lay_weights", compiler_params=room(60),
        cost_estimate=cost(0, 12 * deep * hidden),
    )(w_gate[0], w_up[0], w_down[0])
    before, after = up(own), down(own)
    far_low, far_high = up(before[:half]), down(after[half:])

    whole = pl.BlockSpec(memory_space=pl.ANY)
    vmem = pl.BlockSpec(memory_space=pltpu.VMEM)
    od, saved = pl.pallas_call(
        expert_math,
        in_specs=[pl.BlockSpec(memory_space=pltpu.SMEM)] + [whole] * 6,
        out_specs=[whole, vmem],
        out_shape=[of((rows, 2 * width), BF), of((rows, 3 * hidden), BF)],
        scratch_shapes=[
            pltpu.VMEM((rows, 2 * width), BF), pltpu.VMEM((parts, deep, 3 * hidden), BF), pltpu.VMEM((rows, 2 * width), BF),
            pltpu.SemaphoreType.DMA((2 * parts,)), pltpu.SemaphoreType.DMA((parts + 1,)), pltpu.SemaphoreType.DMA((2 * parts,)),
        ],
        name="expert_math", compiler_params=room(60), cost_estimate=cost(6 * unit, 10 * rows * width),
    )(me, xg, own, after, far_low, far_high, before)
    back = exchange(od)

    grads = pl.pallas_call(
        weight_grads,
        grid_spec=pltpu.PrefetchScalarGridSpec(
            num_scalar_prefetch=1,
            grid=(parts,),
            in_specs=[
                pl.BlockSpec((rows, deep), lambda i, me: (0, lax.rem(me[0] + i, parts))),
                pl.BlockSpec((rows, deep), lambda i, me: (0, lax.rem(me[0] + i, parts) + parts)),
                pl.BlockSpec((rows, 3 * hidden), lambda i, me: (0, 0)),
            ],
            out_specs=pl.BlockSpec((1, deep, 3 * hidden), lambda i, me: (i, 0, 0)),
        ),
        out_shape=of((parts, deep, 3 * hidden), BF),
        name="weight_grads", compiler_params=room(60), cost_estimate=cost(3 * unit, 6 * rows * width),
    )(me, xg, xg, saved)
    low, high = up(grads[2, :half]), down(grads[2, half:])

    def block(n):
        return pl.BlockSpec((1, deep, 3 * hidden), lambda i: (n, 0, 0))

    flat = fixed((deep, 3 * hidden))
    right, left = pl.pallas_call(
        add_far,
        grid=(1,),
        in_specs=[block(1), block(3), fixed((half, 3 * hidden)), fixed((half, 3 * hidden))],
        out_specs=[flat, flat],
        out_shape=[of((deep, 3 * hidden), BF)] * 2,
        name="add_far", compiler_params=room(60), cost_estimate=cost(0, 30 * deep * hidden),
    )(grads, grads, low, high)
    grad_gate, grad_up, grad_down = pl.pallas_call(
        add_last,
        grid=(1,),
        in_specs=[block(0), flat, flat],
        out_specs=[fixed((deep, hidden)), fixed((deep, hidden)), fixed((hidden, deep))],
        out_shape=[of((deep, hidden), BF), of((deep, hidden), BF), of((hidden, deep), BF)],
        name="add_last", compiler_params=room(60), cost_estimate=cost(0, 24 * deep * hidden),
    )(grads, up(right), down(left))
    back, grad_gate, grad_up, grad_down = together(back, grad_gate, grad_up, grad_down)

    mixed, grad_tokens, grad_combine = pl.pallas_call(
        part(merge, slots, experts),
        grid=(width // STEP,),
        in_specs=[
            fixed((top, count)), *[fixed((rows, count))] * 3,
            pl.BlockSpec((count, STEP), lambda i: (0, i)),
            pl.BlockSpec((rows, STEP), lambda i: (0, i)),
            pl.BlockSpec((rows, STEP), lambda i: (0, i + width // STEP)),
        ],
        out_specs=[
            pl.BlockSpec((count, STEP), lambda i: (0, i)), pl.BlockSpec((count, STEP), lambda i: (0, i)), fixed((top, count)),
        ],
        out_shape=[of((count, width), BF), of((count, width), BF), of((top, count), F32)],
        scratch_shapes=[pltpu.VMEM((rows, count), F32)],
        name="merge", compiler_params=room(60), cost_estimate=cost(4 * pick_flops, 5 * rows * width),
    )(ids, *tables, cotangent, back, back)
    return (mixed, grad_tokens, grad_combine.T, grad_gate[None], grad_up[None], grad_down[None])


def solution(mesh):
    rows = P(("dp", "expert"), None)
    deep, wide = P("expert", "dp", None), P("expert", None, "dp")
    return jax.shard_map(
        on_device,
        mesh=mesh,
        in_specs=(rows, rows, rows, rows, P(), deep, deep, wide),
        out_specs=(rows, rows, rows, deep, deep, wide),
        check_vma=False,
    )
```

```python
import functools

import jax
import jax.numpy as jnp
from jax import lax
from jax.experimental import pallas as pl
from jax.experimental.pallas import tpu as pltpu
from jax.sharding import PartitionSpec as P

MIB = 2**20
BF = jnp.bfloat16
F32 = jnp.float32
STEP = 512
MERGE = 1024


def contract(left, right, left_dim, right_dim):
    return lax.dot_general(
        left, right, (((left_dim,), (right_dim,)), ((), ())), preferred_element_type=F32
    )


def together(*arrays):
    return lax.optimization_barrier(arrays)


def hits(ids_ref, cap_ref, slots):
    top, count = ids_ref.shape
    experts = cap_ref.shape[1]
    numbers = lax.broadcasted_iota(jnp.int32, (experts, count), 0)
    chosen = [ids_ref[k : k + 1, :] == numbers for k in range(top)]
    taken = sum(c.astype(F32) for c in chosen)
    earlier = (
        lax.broadcasted_iota(jnp.int32, (count, count), 0)
        < lax.broadcasted_iota(jnp.int32, (count, count), 1)
    ).astype(BF)
    rank = contract(taken.astype(BF), earlier, 1, 0)
    same = lax.broadcasted_iota(jnp.int32, (experts, experts), 0) == lax.broadcasted_iota(
        jnp.int32, (experts, experts), 1
    )
    limit = jnp.sum(jnp.where(same, cap_ref[...].astype(F32), 0.0), axis=1, keepdims=True)
    slot_of = jnp.where((taken > 0.5) & (rank < limit), rank, -1.0)
    wanted = lax.broadcasted_iota(jnp.int32, (experts, slots, count), 1).astype(F32)
    held = (jnp.broadcast_to(slot_of[:, None, :], (experts, slots, count)) == wanted).astype(F32)
    return held.reshape(experts * slots, count), chosen


def shares(held, chosen, comb_ref, slots):
    weights = sum(jnp.where(c, comb_ref[k : k + 1, :], 0.0) for k, c in enumerate(chosen))
    experts, count = weights.shape
    spread = jnp.broadcast_to(weights[:, None, :], (experts, slots, count)).reshape(experts * slots, count)
    return held * spread


def pick_rows(slots, ids_ref, cap_ref, comb_ref, tokens_ref, cot_ref, out_ref, pick_ref, shares_ref, scale_ref):
    i = pl.program_id(0)
    steps = pl.num_programs(0)

    @pl.when(i == 0)
    def _():
        held, chosen = hits(ids_ref, cap_ref, slots)
        pick_ref[...] = held.astype(BF)
        share = shares(held, chosen, comb_ref, slots)
        count = share.shape[1]
        shares_ref[:, :count] = share.astype(BF)
        shares_ref[:, count:] = (share - share.astype(BF).astype(F32)).astype(BF)
        scale = jnp.sum(share, axis=1, keepdims=True)
        scale_ref[...] = jnp.broadcast_to(scale, scale_ref.shape)

    wide = out_ref.shape[1]

    @pl.when(i < steps // 2)
    def _():
        for c in range(0, wide, STEP):
            out_ref[:, c : c + STEP] = contract(pick_ref[...], tokens_ref[:, c : c + STEP], 1, 0).astype(BF)

    @pl.when(i >= steps // 2)
    def _():
        scale = scale_ref[:, :1]
        for c in range(0, wide, STEP):
            rows = contract(pick_ref[...], cot_ref[:, c : c + STEP], 1, 0)
            out_ref[:, c : c + STEP] = (scale * rows).astype(BF)


def lay_weights(gate_ref, up_ref, down_ref, pick_ref, both_ref, out_ref, turned_ref):
    count = pick_ref.shape[1]
    turned_ref[:count, :] = pick_ref[...].T
    turned_ref[count:, :] = both_ref[...].T
    hidden = gate_ref.shape[1]
    out_ref[:, :hidden] = gate_ref[...]
    out_ref[:, hidden : 2 * hidden] = up_ref[...]
    out_ref[:, 2 * hidden :] = down_ref[...].T


def expert_math(
    me_ref, xg_hbm, own_hbm, next_hbm, far_low_hbm, far_high_hbm, prev_hbm, od_hbm, saved_ref, xg_ref, w_ref, od_ref, in_sems, w_sems, out_sems
):
    parts, deep, hidden = w_ref.shape
    hidden //= 3
    half = deep // 2
    order = (0, 1, 3, 2)

    def lanes(n):
        block = lax.rem(me_ref[0] + n % parts, parts) + n // parts * parts
        return pl.ds(pl.multiple_of(block * deep, deep), deep)

    def arrive(n):
        return pltpu.make_async_copy(xg_hbm.at[:, lanes(n)], xg_ref.at[:, pl.ds(n * deep, deep)], in_sems.at[n])

    def leave(n):
        return pltpu.make_async_copy(od_ref.at[:, pl.ds(n * deep, deep)], od_hbm.at[:, lanes(n)], out_sems.at[n])

    def weights(n):
        if n != 2:
            source = {0: own_hbm, 1: next_hbm, 3: prev_hbm}[n]
            return [pltpu.make_async_copy(source, w_ref.at[n], w_sems.at[n])]
        return [
            pltpu.make_async_copy(far_low_hbm, w_ref.at[n, pl.ds(0, half)], w_sems.at[n]),
            pltpu.make_async_copy(far_high_hbm, w_ref.at[n, pl.ds(half, half)], w_sems.at[parts]),
        ]

    for n in order:
        for copy in weights(n):
            copy.start()
        arrive(n).start()
    for n in order:
        arrive(parts + n).start()
    hu = da = 0.0
    for n in order:
        for copy in weights(n):
            copy.wait()
        arrive(n).wait()
        hu = hu + contract(xg_ref[:, n * deep : (n + 1) * deep], w_ref[n, :, : 2 * hidden], 1, 0)
    h, u = hu[:, :hidden], hu[:, hidden:]
    s = jax.nn.sigmoid(h)
    a = (h * s * u).astype(BF)
    saved_ref[:, 2 * hidden :] = a
    for n in order:
        od_ref[:, n * deep : (n + 1) * deep] = contract(a, w_ref[n, :, 2 * hidden :], 1, 1).astype(BF)
        leave(n).start()
    for n in order:
        arrive(parts + n).wait()
        g = xg_ref[:, (parts + n) * deep : (parts + n + 1) * deep]
        da = da + contract(g, w_ref[n, :, 2 * hidden :], 1, 0)
    dh = (da * u * s * (1.0 + h * (1.0 - s))).astype(BF)
    du = (da * h * s).astype(BF)
    saved_ref[:, :hidden] = dh
    saved_ref[:, hidden : 2 * hidden] = du
    both = jnp.concatenate([dh, du], axis=1)
    for n in order:
        m = parts + n
        od_ref[:, m * deep : (m + 1) * deep] = contract(both, w_ref[n, :, : 2 * hidden], 1, 1).astype(BF)
        leave(m).start()
    for n in range(2 * parts):
        leave(n).wait()


def weight_grads(me_ref, x_ref, g_ref, saved_ref, out_ref):
    hidden = out_ref.shape[2] // 3
    out_ref[0, :, : 2 * hidden] = contract(x_ref[...], saved_ref[:, : 2 * hidden], 0, 0).astype(BF)
    out_ref[0, :, 2 * hidden :] = contract(g_ref[...], saved_ref[:, 2 * hidden :], 0, 0).astype(BF)


def add_far(next_ref, prev_ref, low_ref, high_ref, right_ref, left_ref):
    half = low_ref.shape[0]
    right_ref[:half, :] = (next_ref[0, :half, :].astype(F32) + low_ref[...].astype(F32)).astype(BF)
    right_ref[half:, :] = next_ref[0, half:, :]
    left_ref[:half, :] = prev_ref[0, :half, :]
    left_ref[half:, :] = (prev_ref[0, half:, :].astype(F32) + high_ref[...].astype(F32)).astype(BF)


def add_last(own_ref, below_ref, above_ref, gate_ref, up_ref, down_ref):
    hidden = gate_ref.shape[1]
    total = own_ref[0].astype(F32) + below_ref[...].astype(F32) + above_ref[...].astype(F32)
    gate_ref[...] = total[:, :hidden].astype(BF)
    up_ref[...] = total[:, hidden : 2 * hidden].astype(BF)
    down_ref[...] = total[:, 2 * hidden :].astype(BF).T


def merge(
    slots, experts, ids_ref, tables_ref, pick_ref, cot_ref, o_ref, d_ref, mixed_ref, rows_ref, gc_ref, dots_ref
):
    i = pl.program_id(0)

    @pl.when(i == 0)
    def _():
        dots_ref[...] = jnp.zeros(dots_ref.shape, F32)

    o = o_ref[...]
    count = ids_ref.shape[1]
    both = contract(tables_ref[count:, :], o, 1, 0)
    mixed_ref[...] = (both[:count] + both[count:]).astype(BF)
    rows_ref[...] = contract(tables_ref[:count, :], d_ref[...], 1, 0).astype(BF)
    dots_ref[...] += contract(o, cot_ref[...], 1, 1)

    @pl.when(i == pl.num_programs(0) - 1)
    def _():
        top, count = ids_ref.shape
        found = dots_ref[...] * pick_ref[...].astype(F32)
        per_expert = jnp.sum(found.reshape(experts, slots, count), axis=1)
        numbers = lax.broadcasted_iota(jnp.int32, (experts, count), 0)
        for k in range(top):
            hit = ids_ref[k : k + 1, :] == numbers
            gc_ref[k : k + 1, :] = jnp.sum(jnp.where(hit, per_expert, 0.0), axis=0, keepdims=True)


def on_device(tokens, cotangent, expert_ids, combine, capacity, w_gate, w_up, w_down):
    part = functools.partial
    of = jax.ShapeDtypeStruct
    peers = lax.axis_size("expert")
    count, width = tokens.shape
    top = expert_ids.shape[1]
    experts = capacity.shape[0]
    slots = count * top // (2 * peers)
    rows = experts * slots
    hidden = w_gate.shape[2]
    limits = capacity.reshape(1, experts)
    ids, comb = expert_ids.T, combine.T
    unit = 2 * rows * width * hidden
    pick_flops = 2 * rows * count * width

    def cost(flops, moved):
        return pl.CostEstimate(flops=flops, bytes_accessed=moved, transcendentals=0)

    def room(mib):
        return pltpu.CompilerParams(vmem_limit_bytes=mib * MIB)

    def fixed(shape):
        return pl.BlockSpec(shape, lambda i: (0,) * len(shape))

    def exchange(x):
        x = x.reshape(peers, slots, 2 * width)
        return lax.all_to_all(x, "expert", 0, 0, tiled=True).reshape(rows, 2 * width)

    block = width
    sent, pick, both = pl.pallas_call(
        part(pick_rows, slots),
        grid=(2,),
        in_specs=[
            fixed((top, count)), fixed((1, experts)), fixed((top, count)),
            pl.BlockSpec((count, block), lambda i: (0, 0)),
            pl.BlockSpec((count, block), lambda i: (0, 0)),
        ],
        out_specs=[pl.BlockSpec((rows, block), lambda i: (0, i)), fixed((rows, count)), fixed((rows, 2 * count))],
        out_shape=[of((rows, 2 * width), BF), of((rows, count), BF), of((rows, 2 * count), BF)],
        scratch_shapes=[pltpu.VMEM((rows, 128), F32)],
        name="pick_rows", compiler_params=room(60), cost_estimate=cost(2 * pick_flops, 5 * rows * width),
    )(ids, limits, comb, tokens, cotangent)
    xg = exchange(sent)

    parts = lax.axis_size("dp")
    deep = width // parts
    half = deep // 2
    me = lax.axis_index("dp").astype(jnp.int32).reshape(1)

    def up(x):
        return lax.ppermute(x, "dp", [(i, (i + 1) % parts) for i in range(parts)])

    def down(x):
        return lax.ppermute(x, "dp", [(i, (i - 1) % parts) for i in range(parts)])

    own, turned = pl.pallas_call(
        lay_weights, out_shape=[of((deep, 3 * hidden), BF), of((3 * count, rows), BF)], name="lay_weights", compiler_params=room(60),
        cost_estimate=cost(0, 12 * deep * hidden),
    )(w_gate[0], w_up[0], w_down[0], pick, both)
    before, after = up(own), down(own)
    far_low, far_high = up(before[:half]), down(after[half:])

    whole = pl.BlockSpec(memory_space=pl.ANY)
    vmem = pl.BlockSpec(memory_space=pltpu.VMEM)
    od, saved = pl.pallas_call(
        expert_math,
        in_specs=[pl.BlockSpec(memory_space=pltpu.SMEM)] + [whole] * 6,
        out_specs=[whole, vmem],
        out_shape=[of((rows, 2 * width), BF), of((rows, 3 * hidden), BF)],
        scratch_shapes=[
            pltpu.VMEM((rows, 2 * width), BF), pltpu.VMEM((parts, deep, 3 * hidden), BF), pltpu.VMEM((rows, 2 * width), BF),
            pltpu.SemaphoreType.DMA((2 * parts,)), pltpu.SemaphoreType.DMA((parts + 1,)), pltpu.SemaphoreType.DMA((2 * parts,)),
        ],
        name="expert_math", compiler_params=room(60), cost_estimate=cost(6 * unit, 10 * rows * width),
    )(me, xg, own, after, far_low, far_high, before)
    back = exchange(od)

    grads = pl.pallas_call(
        weight_grads,
        grid_spec=pltpu.PrefetchScalarGridSpec(
            num_scalar_prefetch=1,
            grid=(parts,),
            in_specs=[
                pl.BlockSpec((rows, deep), lambda i, me: (0, lax.rem(me[0] + i, parts))),
                pl.BlockSpec((rows, deep), lambda i, me: (0, lax.rem(me[0] + i, parts) + parts)),
                pl.BlockSpec((rows, 3 * hidden), lambda i, me: (0, 0)),
            ],
            out_specs=pl.BlockSpec((1, deep, 3 * hidden), lambda i, me: (i, 0, 0)),
        ),
        out_shape=of((parts, deep, 3 * hidden), BF),
        name="weight_grads", compiler_params=room(60), cost_estimate=cost(3 * unit, 6 * rows * width),
    )(me, xg, xg, saved)
    low, high = up(grads[2, :half]), down(grads[2, half:])

    def block(n):
        return pl.BlockSpec((1, deep, 3 * hidden), lambda i: (n, 0, 0))

    flat = fixed((deep, 3 * hidden))
    right, left = pl.pallas_call(
        add_far,
        grid=(1,),
        in_specs=[block(1), block(3), fixed((half, 3 * hidden)), fixed((half, 3 * hidden))],
        out_specs=[flat, flat],
        out_shape=[of((deep, 3 * hidden), BF)] * 2,
        name="add_far", compiler_params=room(60), cost_estimate=cost(0, 30 * deep * hidden),
    )(grads, grads, low, high)
    grad_gate, grad_up, grad_down = pl.pallas_call(
        add_last,
        grid=(1,),
        in_specs=[block(0), flat, flat],
        out_specs=[fixed((deep, hidden)), fixed((deep, hidden)), fixed((hidden, deep))],
        out_shape=[of((deep, hidden), BF), of((deep, hidden), BF), of((hidden, deep), BF)],
        name="add_last", compiler_params=room(60), cost_estimate=cost(0, 24 * deep * hidden),
    )(grads, up(right), down(left))
    back, grad_gate, grad_up, grad_down = together(back, grad_gate, grad_up, grad_down)

    mixed, grad_tokens, grad_combine = pl.pallas_call(
        part(merge, slots, experts),
        grid=(width // MERGE,),
        in_specs=[
            fixed((top, count)), fixed((3 * count, rows)), fixed((rows, count)),
            pl.BlockSpec((count, MERGE), lambda i: (0, i)),
            pl.BlockSpec((rows, MERGE), lambda i: (0, i)),
            pl.BlockSpec((rows, MERGE), lambda i: (0, i + width // MERGE)),
        ],
        out_specs=[
            pl.BlockSpec((count, MERGE), lambda i: (0, i)), pl.BlockSpec((count, MERGE), lambda i: (0, i)), fixed((top, count)),
        ],
        out_shape=[of((count, width), BF), of((count, width), BF), of((top, count), F32)],
        scratch_shapes=[pltpu.VMEM((rows, count), F32)],
        name="merge", compiler_params=room(60), cost_estimate=cost(4 * pick_flops, 5 * rows * width),
    )(ids, turned, pick, cotangent, back, back)
    return (mixed, grad_tokens, grad_combine.T, grad_gate[None], grad_up[None], grad_down[None])


def solution(mesh):
    rows = P(("dp", "expert"), None)
    deep, wide = P("expert", "dp", None), P("expert", None, "dp")
    return jax.shard_map(
        on_device,
        mesh=mesh,
        in_specs=(rows, rows, rows, rows, P(), deep, deep, wide),
        out_specs=(rows, rows, rows, deep, deep, wide),
        check_vma=False,
    )
```

```python
import functools

import jax
import jax.numpy as jnp
from jax import lax
from jax.experimental import pallas as pl
from jax.experimental.pallas import tpu as pltpu
from jax.sharding import PartitionSpec as P

MIB = 2**20
BF = jnp.bfloat16
F32 = jnp.float32
STEP = 512


def contract(left, right, left_dim, right_dim):
    return lax.dot_general(
        left, right, (((left_dim,), (right_dim,)), ((), ())), preferred_element_type=F32
    )


def together(*arrays):
    return lax.optimization_barrier(arrays)


def hits(ids_ref, cap_ref, slots):
    top, count = ids_ref.shape
    experts = cap_ref.shape[1]
    numbers = lax.broadcasted_iota(jnp.int32, (experts, count), 0)
    chosen = [ids_ref[k : k + 1, :] == numbers for k in range(top)]
    taken = sum(c.astype(F32) for c in chosen)
    earlier = (
        lax.broadcasted_iota(jnp.int32, (count, count), 0)
        < lax.broadcasted_iota(jnp.int32, (count, count), 1)
    ).astype(BF)
    rank = contract(taken.astype(BF), earlier, 1, 0)
    same = lax.broadcasted_iota(jnp.int32, (experts, experts), 0) == lax.broadcasted_iota(
        jnp.int32, (experts, experts), 1
    )
    limit = jnp.sum(jnp.where(same, cap_ref[...].astype(F32), 0.0), axis=1, keepdims=True)
    slot_of = jnp.where((taken > 0.5) & (rank < limit), rank, -1.0)
    wanted = lax.broadcasted_iota(jnp.int32, (experts, slots, count), 1).astype(F32)
    held = (jnp.broadcast_to(slot_of[:, None, :], (experts, slots, count)) == wanted).astype(F32)
    return held.reshape(experts * slots, count), chosen


def shares(held, chosen, comb_ref, slots):
    weights = sum(jnp.where(c, comb_ref[k : k + 1, :], 0.0) for k, c in enumerate(chosen))
    experts, count = weights.shape
    spread = jnp.broadcast_to(weights[:, None, :], (experts, slots, count)).reshape(experts * slots, count)
    return held * spread


def pick_rows(
    slots, ids_ref, cap_ref, comb_ref, tokens_hbm, cot_hbm, out_hbm, pick_ref, shares_ref, in_ref, out_ref, in_sems, out_sems
):
    count, width = tokens_hbm.shape
    pieces = [slice(c, c + STEP) for c in range(0, 2 * width, STEP)]

    def arrive(n):
        source, at = (tokens_hbm, n * STEP) if n * STEP < width else (cot_hbm, n * STEP - width)
        return pltpu.make_async_copy(source.at[:, pl.ds(at, STEP)], in_ref.at[:, pl.ds(n * STEP, STEP)], in_sems.at[n])

    def leave(n):
        at = pl.ds(n * STEP, STEP)
        return pltpu.make_async_copy(out_ref.at[:, at], out_hbm.at[:, at], out_sems.at[n])

    for n in range(len(pieces)):
        arrive(n).start()
    held, chosen = hits(ids_ref, cap_ref, slots)
    pick = held.astype(BF)
    share = shares(held, chosen, comb_ref, slots)
    pick_ref[...] = pick
    shares_ref[:, :count] = share.astype(BF)
    shares_ref[:, count:] = (share - share.astype(BF).astype(F32)).astype(BF)
    scale = jnp.sum(share, axis=1, keepdims=True)
    for n, piece in enumerate(pieces):
        arrive(n).wait()
        rows = contract(pick, in_ref[:, piece], 1, 0)
        if n * STEP >= width:
            rows = scale * rows
        out_ref[:, piece] = rows.astype(BF)
        leave(n).start()
    for n in range(len(pieces)):
        leave(n).wait()


def lay_weights(gate_ref, up_ref, down_ref, pick_ref, both_ref, out_ref, turned_ref):
    count = pick_ref.shape[1]
    turned_ref[:count, :] = pick_ref[...].T
    turned_ref[count:, :] = both_ref[...].T
    hidden = gate_ref.shape[1]
    out_ref[:, :hidden] = gate_ref[...]
    out_ref[:, hidden : 2 * hidden] = up_ref[...]
    out_ref[:, 2 * hidden :] = down_ref[...].T


def expert_math(
    me_ref, xg_hbm, own_hbm, next_hbm, far_low_hbm, far_high_hbm, prev_hbm, od_hbm, saved_ref, xg_ref, w_ref, od_ref, in_sems, w_sems, out_sems
):
    parts, deep, hidden = w_ref.shape
    hidden //= 3
    half = deep // 2
    order = (0, 1, 3, 2)

    def lanes(n):
        block = lax.rem(me_ref[0] + n % parts, parts) + n // parts * parts
        return pl.ds(pl.multiple_of(block * deep, deep), deep)

    def arrive(n):
        return pltpu.make_async_copy(xg_hbm.at[:, lanes(n)], xg_ref.at[:, pl.ds(n * deep, deep)], in_sems.at[n])

    def leave(n):
        return pltpu.make_async_copy(od_ref.at[:, pl.ds(n * deep, deep)], od_hbm.at[:, lanes(n)], out_sems.at[n])

    def weights(n):
        if n != 2:
            source = {0: own_hbm, 1: next_hbm, 3: prev_hbm}[n]
            return [pltpu.make_async_copy(source, w_ref.at[n], w_sems.at[n])]
        return [
            pltpu.make_async_copy(far_low_hbm, w_ref.at[n, pl.ds(0, half)], w_sems.at[n]),
            pltpu.make_async_copy(far_high_hbm, w_ref.at[n, pl.ds(half, half)], w_sems.at[parts]),
        ]

    for n in order:
        for copy in weights(n):
            copy.start()
        arrive(n).start()
    for n in order:
        arrive(parts + n).start()
    hu = da = 0.0
    for n in order:
        for copy in weights(n):
            copy.wait()
        arrive(n).wait()
        hu = hu + contract(xg_ref[:, n * deep : (n + 1) * deep], w_ref[n, :, : 2 * hidden], 1, 0)
    h, u = hu[:, :hidden], hu[:, hidden:]
    s = jax.nn.sigmoid(h)
    a = (h * s * u).astype(BF)
    saved_ref[:, 2 * hidden :] = a
    for n in order:
        od_ref[:, n * deep : (n + 1) * deep] = contract(a, w_ref[n, :, 2 * hidden :], 1, 1).astype(BF)
        leave(n).start()
    for n in order:
        arrive(parts + n).wait()
        g = xg_ref[:, (parts + n) * deep : (parts + n + 1) * deep]
        da = da + contract(g, w_ref[n, :, 2 * hidden :], 1, 0)
    dh = (da * u * s * (1.0 + h * (1.0 - s))).astype(BF)
    du = (da * h * s).astype(BF)
    saved_ref[:, :hidden] = dh
    saved_ref[:, hidden : 2 * hidden] = du
    both = jnp.concatenate([dh, du], axis=1)
    for n in order:
        m = parts + n
        od_ref[:, m * deep : (m + 1) * deep] = contract(both, w_ref[n, :, : 2 * hidden], 1, 1).astype(BF)
        leave(m).start()
    for n in range(2 * parts):
        leave(n).wait()


def weight_grads(me_ref, x_ref, g_ref, saved_ref, out_ref):
    hidden = out_ref.shape[2] // 3
    out_ref[0, :, : 2 * hidden] = contract(x_ref[...], saved_ref[:, : 2 * hidden], 0, 0).astype(BF)
    out_ref[0, :, 2 * hidden :] = contract(g_ref[...], saved_ref[:, 2 * hidden :], 0, 0).astype(BF)


def add_far(next_ref, prev_ref, low_ref, high_ref, right_ref, left_ref):
    half = low_ref.shape[0]
    right_ref[:half, :] = (next_ref[0, :half, :].astype(F32) + low_ref[...].astype(F32)).astype(BF)
    right_ref[half:, :] = next_ref[0, half:, :]
    left_ref[:half, :] = prev_ref[0, :half, :]
    left_ref[half:, :] = (prev_ref[0, half:, :].astype(F32) + high_ref[...].astype(F32)).astype(BF)


def add_last(own_ref, below_ref, above_ref, gate_ref, up_ref, down_ref):
    hidden = gate_ref.shape[1]
    total = own_ref[0].astype(F32) + below_ref[...].astype(F32) + above_ref[...].astype(F32)
    gate_ref[...] = total[:, :hidden].astype(BF)
    up_ref[...] = total[:, hidden : 2 * hidden].astype(BF)
    down_ref[...] = total[:, 2 * hidden :].astype(BF).T


def merge(
    slots, experts, ids_ref, tables_hbm, pick_hbm, cot_hbm, back_hbm, mixed_hbm, rows_hbm, gc_ref,
    tables_ref, pick_ref, cot_ref, back_ref, mixed_ref, rows_ref, table_sems, cot_sems, in_sems, out_sems
):
    top, count = ids_ref.shape
    width = cot_hbm.shape[1]
    steps = width // STEP
    tables = [
        pltpu.make_async_copy(tables_hbm, tables_ref, table_sems.at[0]),
        pltpu.make_async_copy(pick_hbm, pick_ref, table_sems.at[1]),
    ]

    def at(n):
        return pl.ds(n * STEP, STEP)

    def arrive(n):
        return pltpu.make_async_copy(back_hbm.at[:, at(n)], back_ref.at[:, at(n)], in_sems.at[n])

    def cot(n):
        return pltpu.make_async_copy(cot_hbm.at[:, at(n)], cot_ref.at[:, at(n)], cot_sems.at[n])

    def leave(n):
        from_ref, to_hbm, m = (mixed_ref, mixed_hbm, n) if n < steps else (rows_ref, rows_hbm, n - steps)
        return pltpu.make_async_copy(from_ref.at[:, at(m)], to_hbm.at[:, at(m)], out_sems.at[n])

    tables[0].start()
    for n in range(steps):
        arrive(n).start()
        cot(n).start()
        arrive(steps + n).start()
    tables[1].start()
    tables[0].wait()
    dots = 0.0
    for n in range(steps):
        piece = slice(n * STEP, (n + 1) * STEP)
        arrive(n).wait()
        o = back_ref[:, piece]
        both = contract(tables_ref[count:, :], o, 1, 0)
        mixed_ref[:, piece] = (both[:count] + both[count:]).astype(BF)
        leave(n).start()
        cot(n).wait()
        dots = dots + contract(o, cot_ref[:, piece], 1, 1)
        arrive(steps + n).wait()
        d = back_ref[:, width + n * STEP : width + (n + 1) * STEP]
        rows_ref[:, piece] = contract(tables_ref[:count, :], d, 1, 0).astype(BF)
        leave(steps + n).start()
    tables[1].wait()
    found = dots * pick_ref[...].astype(F32)
    per_expert = jnp.sum(found.reshape(experts, slots, count), axis=1)
    numbers = lax.broadcasted_iota(jnp.int32, (experts, count), 0)
    for k in range(top):
        hit = ids_ref[k : k + 1, :] == numbers
        gc_ref[k : k + 1, :] = jnp.sum(jnp.where(hit, per_expert, 0.0), axis=0, keepdims=True)
    for n in range(2 * steps):
        leave(n).wait()


def on_device(tokens, cotangent, expert_ids, combine, capacity, w_gate, w_up, w_down):
    part = functools.partial
    of = jax.ShapeDtypeStruct
    peers = lax.axis_size("expert")
    count, width = tokens.shape
    top = expert_ids.shape[1]
    experts = capacity.shape[0]
    slots = count * top // (2 * peers)
    rows = experts * slots
    hidden = w_gate.shape[2]
    limits = capacity.reshape(1, experts)
    ids, comb = expert_ids.T, combine.T
    unit = 2 * rows * width * hidden
    pick_flops = 2 * rows * count * width

    def cost(flops, moved):
        return pl.CostEstimate(flops=flops, bytes_accessed=moved, transcendentals=0)

    def room(mib):
        return pltpu.CompilerParams(vmem_limit_bytes=mib * MIB)

    def fixed(shape):
        return pl.BlockSpec(shape, lambda i: (0,) * len(shape))

    def exchange(x):
        x = x.reshape(peers, slots, 2 * width)
        return lax.all_to_all(x, "expert", 0, 0, tiled=True).reshape(rows, 2 * width)

    whole = pl.BlockSpec(memory_space=pl.ANY)
    vmem = pl.BlockSpec(memory_space=pltpu.VMEM)
    copies = pltpu.SemaphoreType.DMA
    pieces = 2 * width // STEP
    sent, pick, both = pl.pallas_call(
        part(pick_rows, slots),
        in_specs=[vmem, vmem, vmem, whole, whole],
        out_specs=[whole, vmem, vmem],
        out_shape=[of((rows, 2 * width), BF), of((rows, count), BF), of((rows, 2 * count), BF)],
        scratch_shapes=[
            pltpu.VMEM((count, 2 * width), BF), pltpu.VMEM((rows, 2 * width), BF), copies((pieces,)), copies((pieces,)),
        ],
        name="pick_rows", compiler_params=room(60), cost_estimate=cost(2 * pick_flops, 5 * rows * width),
    )(ids, limits, comb, tokens, cotangent)
    xg = exchange(sent)

    parts = lax.axis_size("dp")
    deep = width // parts
    half = deep // 2
    me = lax.axis_index("dp").astype(jnp.int32).reshape(1)

    def up(x):
        return lax.ppermute(x, "dp", [(i, (i + 1) % parts) for i in range(parts)])

    def down(x):
        return lax.ppermute(x, "dp", [(i, (i - 1) % parts) for i in range(parts)])

    own, turned = pl.pallas_call(
        lay_weights, out_shape=[of((deep, 3 * hidden), BF), of((3 * count, rows), BF)], name="lay_weights", compiler_params=room(60),
        cost_estimate=cost(0, 12 * deep * hidden),
    )(w_gate[0], w_up[0], w_down[0], pick, both)
    before, after = up(own), down(own)
    far_low, far_high = up(before[:half]), down(after[half:])

    od, saved = pl.pallas_call(
        expert_math,
        in_specs=[pl.BlockSpec(memory_space=pltpu.SMEM)] + [whole] * 6,
        out_specs=[whole, vmem],
        out_shape=[of((rows, 2 * width), BF), of((rows, 3 * hidden), BF)],
        scratch_shapes=[
            pltpu.VMEM((rows, 2 * width), BF), pltpu.VMEM((parts, deep, 3 * hidden), BF), pltpu.VMEM((rows, 2 * width), BF),
            pltpu.SemaphoreType.DMA((2 * parts,)), pltpu.SemaphoreType.DMA((parts + 1,)), pltpu.SemaphoreType.DMA((2 * parts,)),
        ],
        name="expert_math", compiler_params=room(60), cost_estimate=cost(6 * unit, 10 * rows * width),
    )(me, xg, own, after, far_low, far_high, before)
    back = exchange(od)

    grads = pl.pallas_call(
        weight_grads,
        grid_spec=pltpu.PrefetchScalarGridSpec(
            num_scalar_prefetch=1,
            grid=(parts,),
            in_specs=[
                pl.BlockSpec((rows, deep), lambda i, me: (0, lax.rem(me[0] + i, parts))),
                pl.BlockSpec((rows, deep), lambda i, me: (0, lax.rem(me[0] + i, parts) + parts)),
                pl.BlockSpec((rows, 3 * hidden), lambda i, me: (0, 0)),
            ],
            out_specs=pl.BlockSpec((1, deep, 3 * hidden), lambda i, me: (i, 0, 0)),
        ),
        out_shape=of((parts, deep, 3 * hidden), BF),
        name="weight_grads", compiler_params=room(60), cost_estimate=cost(3 * unit, 6 * rows * width),
    )(me, xg, xg, saved)
    low, high = up(grads[2, :half]), down(grads[2, half:])

    def block(n):
        return pl.BlockSpec((1, deep, 3 * hidden), lambda i: (n, 0, 0))

    flat = fixed((deep, 3 * hidden))
    right, left = pl.pallas_call(
        add_far,
        grid=(1,),
        in_specs=[block(1), block(3), fixed((half, 3 * hidden)), fixed((half, 3 * hidden))],
        out_specs=[flat, flat],
        out_shape=[of((deep, 3 * hidden), BF)] * 2,
        name="add_far", compiler_params=room(60), cost_estimate=cost(0, 30 * deep * hidden),
    )(grads, grads, low, high)
    grad_gate, grad_up, grad_down = pl.pallas_call(
        add_last,
        grid=(1,),
        in_specs=[block(0), flat, flat],
        out_specs=[fixed((deep, hidden)), fixed((deep, hidden)), fixed((hidden, deep))],
        out_shape=[of((deep, hidden), BF), of((deep, hidden), BF), of((hidden, deep), BF)],
        name="add_last", compiler_params=room(60), cost_estimate=cost(0, 24 * deep * hidden),
    )(grads, up(right), down(left))
    back, grad_gate, grad_up, grad_down = together(back, grad_gate, grad_up, grad_down)

    mixed, grad_tokens, grad_combine = pl.pallas_call(
        part(merge, slots, experts),
        in_specs=[vmem] + [whole] * 4,
        out_specs=[whole, whole, vmem],
        out_shape=[of((count, width), BF), of((count, width), BF), of((top, count), F32)],
        scratch_shapes=[
            pltpu.VMEM((3 * count, rows), BF), pltpu.VMEM((rows, count), BF), pltpu.VMEM((count, width), BF),
            pltpu.VMEM((rows, 2 * width), BF), pltpu.VMEM((count, width), BF), pltpu.VMEM((count, width), BF),
            copies((2,)), copies((pieces // 2,)), copies((pieces,)), copies((pieces,)),
        ],
        name="merge", compiler_params=room(60), cost_estimate=cost(4 * pick_flops, 5 * rows * width),
    )(ids, turned, pick, cotangent, back)
    return (mixed, grad_tokens, grad_combine.T, grad_gate[None], grad_up[None], grad_down[None])


def solution(mesh):
    rows = P(("dp", "expert"), None)
    deep, wide = P("expert", "dp", None), P("expert", None, "dp")
    return jax.shard_map(
        on_device,
        mesh=mesh,
        in_specs=(rows, rows, rows, rows, P(), deep, deep, wide),
        out_specs=(rows, rows, rows, deep, deep, wide),
        check_vma=False,
    )
```

```python
import functools

import jax
import jax.numpy as jnp
from jax import lax
from jax.experimental import pallas as pl
from jax.experimental.pallas import tpu as pltpu
from jax.sharding import PartitionSpec as P

MIB = 2**20
BF = jnp.bfloat16
F32 = jnp.float32
STEP = 512
MERGE = 1024


def contract(left, right, left_dim, right_dim):
    return lax.dot_general(
        left, right, (((left_dim,), (right_dim,)), ((), ())), preferred_element_type=F32
    )


def together(*arrays):
    return lax.optimization_barrier(arrays)


def hits(ids_ref, cap_ref, slots):
    top, count = ids_ref.shape
    experts = cap_ref.shape[1]
    numbers = lax.broadcasted_iota(jnp.int32, (experts, count), 0)
    chosen = [ids_ref[k : k + 1, :] == numbers for k in range(top)]
    taken = sum(c.astype(F32) for c in chosen)
    earlier = (
        lax.broadcasted_iota(jnp.int32, (count, count), 0)
        < lax.broadcasted_iota(jnp.int32, (count, count), 1)
    ).astype(BF)
    rank = contract(taken.astype(BF), earlier, 1, 0)
    same = lax.broadcasted_iota(jnp.int32, (experts, experts), 0) == lax.broadcasted_iota(
        jnp.int32, (experts, experts), 1
    )
    limit = jnp.sum(jnp.where(same, cap_ref[...].astype(F32), 0.0), axis=1, keepdims=True)
    slot_of = jnp.where((taken > 0.5) & (rank < limit), rank, -1.0)
    wanted = lax.broadcasted_iota(jnp.int32, (experts, slots, count), 1).astype(F32)
    held = (jnp.broadcast_to(slot_of[:, None, :], (experts, slots, count)) == wanted).astype(F32)
    return held.reshape(experts * slots, count), chosen


def shares(held, chosen, comb_ref, slots):
    weights = sum(jnp.where(c, comb_ref[k : k + 1, :], 0.0) for k, c in enumerate(chosen))
    experts, count = weights.shape
    spread = jnp.broadcast_to(weights[:, None, :], (experts, slots, count)).reshape(experts * slots, count)
    return held * spread


def pick_rows(slots, ids_ref, cap_ref, comb_ref, tokens_ref, cot_ref, out_ref, pick_ref, shares_ref, scale_ref):
    i = pl.program_id(0)
    steps = pl.num_programs(0)

    @pl.when(i == 0)
    def _():
        held, chosen = hits(ids_ref, cap_ref, slots)
        pick_ref[...] = held.astype(BF)
        share = shares(held, chosen, comb_ref, slots)
        count = share.shape[1]
        shares_ref[:, :count] = share.astype(BF)
        shares_ref[:, count:] = (share - share.astype(BF).astype(F32)).astype(BF)
        scale = jnp.sum(share, axis=1, keepdims=True)
        scale_ref[...] = jnp.broadcast_to(scale, scale_ref.shape)

    wide = out_ref.shape[1]

    @pl.when(i < steps // 2)
    def _():
        for c in range(0, wide, STEP):
            out_ref[:, c : c + STEP] = contract(pick_ref[...], tokens_ref[:, c : c + STEP], 1, 0).astype(BF)

    @pl.when(i >= steps // 2)
    def _():
        scale = scale_ref[:, :1]
        for c in range(0, wide, STEP):
            rows = contract(pick_ref[...], cot_ref[:, c : c + STEP], 1, 0)
            out_ref[:, c : c + STEP] = (scale * rows).astype(BF)


def lay_weights(gate_ref, up_ref, down_ref, pick_ref, both_ref, out_ref, turned_ref):
    count = pick_ref.shape[1]
    turned_ref[:count, :] = pick_ref[...].T
    turned_ref[count:, :] = both_ref[...].T
    hidden = gate_ref.shape[1]
    out_ref[:, :hidden] = gate_ref[...]
    out_ref[:, hidden : 2 * hidden] = up_ref[...]
    out_ref[:, 2 * hidden :] = down_ref[...].T


def expert_math(
    me_ref, xg_hbm, own_hbm, next_hbm, far_low_ref, far_high_ref, prev_hbm, od_hbm, saved_ref, xg_ref, w_ref, od_ref, in_sems, w_sems, out_sems
):
    deep, hidden = own_hbm.shape
    hidden //= 3
    parts = od_ref.shape[1] // (2 * deep)
    half = deep // 2
    order = (2, 0, 1, 3)

    def lanes(n):
        block = lax.rem(me_ref[0] + n % parts, parts) + n // parts * parts
        return pl.ds(pl.multiple_of(block * deep, deep), deep)

    def arrive(n):
        return pltpu.make_async_copy(xg_hbm.at[:, lanes(n)], xg_ref.at[:, pl.ds(n * deep, deep)], in_sems.at[n])

    def leave(n):
        return pltpu.make_async_copy(od_ref.at[:, pl.ds(n * deep, deep)], od_hbm.at[:, lanes(n)], out_sems.at[n])

    places = {0: 0, 1: 1, 3: 2}
    sources = {0: own_hbm, 1: next_hbm, 3: prev_hbm}
    moved = {n: pltpu.make_async_copy(sources[n], w_ref.at[p], w_sems.at[p]) for n, p in places.items()}

    def pieces(n):
        if n == 2:
            return [(0, far_low_ref), (half, far_high_ref)]
        return [(0, w_ref.at[places[n]])]

    for n in order:
        arrive(n).start()
        if n in moved:
            moved[n].start()
    for n in order:
        arrive(parts + n).start()
    hu = da = 0.0
    for n in order:
        arrive(n).wait()
        if n in moved:
            moved[n].wait()
        for start, w in pieces(n):
            at = n * deep + start
            hu = hu + contract(xg_ref[:, at : at + w.shape[0]], w[:, : 2 * hidden], 1, 0)
    h, u = hu[:, :hidden], hu[:, hidden:]
    s = jax.nn.sigmoid(h)
    a = (h * s * u).astype(BF)
    saved_ref[:, 2 * hidden :] = a
    for n in order:
        for start, w in pieces(n):
            at = n * deep + start
            od_ref[:, at : at + w.shape[0]] = contract(a, w[:, 2 * hidden :], 1, 1).astype(BF)
        leave(n).start()
    for n in order:
        arrive(parts + n).wait()
        for start, w in pieces(n):
            at = (parts + n) * deep + start
            da = da + contract(xg_ref[:, at : at + w.shape[0]], w[:, 2 * hidden :], 1, 0)
    dh = (da * u * s * (1.0 + h * (1.0 - s))).astype(BF)
    du = (da * h * s).astype(BF)
    saved_ref[:, :hidden] = dh
    saved_ref[:, hidden : 2 * hidden] = du
    both = jnp.concatenate([dh, du], axis=1)
    for n in order:
        m = parts + n
        for start, w in pieces(n):
            at = m * deep + start
            od_ref[:, at : at + w.shape[0]] = contract(both, w[:, : 2 * hidden], 1, 1).astype(BF)
        leave(m).start()
    for n in range(2 * parts):
        leave(n).wait()


def weight_grads(me_ref, x_ref, g_ref, saved_ref, out_ref):
    hidden = out_ref.shape[2] // 3
    out_ref[0, :, : 2 * hidden] = contract(x_ref[...], saved_ref[:, : 2 * hidden], 0, 0).astype(BF)
    out_ref[0, :, 2 * hidden :] = contract(g_ref[...], saved_ref[:, 2 * hidden :], 0, 0).astype(BF)


def add_far(next_ref, prev_ref, low_ref, high_ref, right_ref, left_ref):
    half = low_ref.shape[0]
    right_ref[:half, :] = (next_ref[0, :half, :].astype(F32) + low_ref[...].astype(F32)).astype(BF)
    right_ref[half:, :] = next_ref[0, half:, :]
    left_ref[:half, :] = prev_ref[0, :half, :]
    left_ref[half:, :] = (prev_ref[0, half:, :].astype(F32) + high_ref[...].astype(F32)).astype(BF)


def add_last(own_ref, below_ref, above_ref, gate_ref, up_ref, down_ref):
    hidden = gate_ref.shape[1]
    total = own_ref[0].astype(F32) + below_ref[...].astype(F32) + above_ref[...].astype(F32)
    gate_ref[...] = total[:, :hidden].astype(BF)
    up_ref[...] = total[:, hidden : 2 * hidden].astype(BF)
    down_ref[...] = total[:, 2 * hidden :].astype(BF).T


def merge(
    slots, experts, ids_ref, tables_ref, pick_ref, cot_ref, o_ref, d_ref, mixed_ref, rows_ref, gc_ref, dots_ref
):
    i = pl.program_id(0)

    @pl.when(i == 0)
    def _():
        dots_ref[...] = jnp.zeros(dots_ref.shape, F32)

    o = o_ref[...]
    count = ids_ref.shape[1]
    both = contract(tables_ref[count:, :], o, 1, 0)
    mixed_ref[...] = (both[:count] + both[count:]).astype(BF)
    rows_ref[...] = contract(tables_ref[:count, :], d_ref[...], 1, 0).astype(BF)
    dots_ref[...] += contract(o, cot_ref[...], 1, 1)

    @pl.when(i == pl.num_programs(0) - 1)
    def _():
        top, count = ids_ref.shape
        found = dots_ref[...] * pick_ref[...].astype(F32)
        per_expert = jnp.sum(found.reshape(experts, slots, count), axis=1)
        numbers = lax.broadcasted_iota(jnp.int32, (experts, count), 0)
        for k in range(top):
            hit = ids_ref[k : k + 1, :] == numbers
            gc_ref[k : k + 1, :] = jnp.sum(jnp.where(hit, per_expert, 0.0), axis=0, keepdims=True)


def on_device(tokens, cotangent, expert_ids, combine, capacity, w_gate, w_up, w_down):
    part = functools.partial
    of = jax.ShapeDtypeStruct
    peers = lax.axis_size("expert")
    count, width = tokens.shape
    top = expert_ids.shape[1]
    experts = capacity.shape[0]
    slots = count * top // (2 * peers)
    rows = experts * slots
    hidden = w_gate.shape[2]
    limits = capacity.reshape(1, experts)
    ids, comb = expert_ids.T, combine.T
    unit = 2 * rows * width * hidden
    pick_flops = 2 * rows * count * width

    def cost(flops, moved):
        return pl.CostEstimate(flops=flops, bytes_accessed=moved, transcendentals=0)

    def room(mib):
        return pltpu.CompilerParams(vmem_limit_bytes=mib * MIB)

    def fixed(shape):
        return pl.BlockSpec(shape, lambda i: (0,) * len(shape))

    def exchange(x):
        x = x.reshape(peers, slots, 2 * width)
        return lax.all_to_all(x, "expert", 0, 0, tiled=True).reshape(rows, 2 * width)

    block = width
    sent, pick, both = pl.pallas_call(
        part(pick_rows, slots),
        grid=(2,),
        in_specs=[
            fixed((top, count)), fixed((1, experts)), fixed((top, count)),
            pl.BlockSpec((count, block), lambda i: (0, 0)),
            pl.BlockSpec((count, block), lambda i: (0, 0)),
        ],
        out_specs=[pl.BlockSpec((rows, block), lambda i: (0, i)), fixed((rows, count)), fixed((rows, 2 * count))],
        out_shape=[of((rows, 2 * width), BF), of((rows, count), BF), of((rows, 2 * count), BF)],
        scratch_shapes=[pltpu.VMEM((rows, 128), F32)],
        name="pick_rows", compiler_params=room(60), cost_estimate=cost(2 * pick_flops, 5 * rows * width),
    )(ids, limits, comb, tokens, cotangent)
    xg = exchange(sent)

    parts = lax.axis_size("dp")
    deep = width // parts
    half = deep // 2
    me = lax.axis_index("dp").astype(jnp.int32).reshape(1)

    def up(x):
        return lax.ppermute(x, "dp", [(i, (i + 1) % parts) for i in range(parts)])

    def down(x):
        return lax.ppermute(x, "dp", [(i, (i - 1) % parts) for i in range(parts)])

    own, turned = pl.pallas_call(
        lay_weights, out_shape=[of((deep, 3 * hidden), BF), of((3 * count, rows), BF)], name="lay_weights", compiler_params=room(60),
        cost_estimate=cost(0, 12 * deep * hidden),
    )(w_gate[0], w_up[0], w_down[0], pick, both)
    before, after = up(own), down(own)
    far_low, far_high = up(before[:half]), down(after[half:])

    whole = pl.BlockSpec(memory_space=pl.ANY)
    vmem = pl.BlockSpec(memory_space=pltpu.VMEM)
    od, saved = pl.pallas_call(
        expert_math,
        in_specs=[pl.BlockSpec(memory_space=pltpu.SMEM), whole, whole, whole, vmem, vmem, whole],
        out_specs=[whole, vmem],
        out_shape=[of((rows, 2 * width), BF), of((rows, 3 * hidden), BF)],
        scratch_shapes=[
            pltpu.VMEM((rows, 2 * width), BF), pltpu.VMEM((3, deep, 3 * hidden), BF), pltpu.VMEM((rows, 2 * width), BF),
            pltpu.SemaphoreType.DMA((2 * parts,)), pltpu.SemaphoreType.DMA((3,)), pltpu.SemaphoreType.DMA((2 * parts,)),
        ],
        name="expert_math", compiler_params=room(51), cost_estimate=cost(6 * unit, 10 * rows * width),
    )(me, xg, own, after, far_low, far_high, before)
    back = exchange(od)

    grads = pl.pallas_call(
        weight_grads,
        grid_spec=pltpu.PrefetchScalarGridSpec(
            num_scalar_prefetch=1,
            grid=(parts,),
            in_specs=[
                pl.BlockSpec((rows, deep), lambda i, me: (0, lax.rem(me[0] + i, parts))),
                pl.BlockSpec((rows, deep), lambda i, me: (0, lax.rem(me[0] + i, parts) + parts)),
                pl.BlockSpec((rows, 3 * hidden), lambda i, me: (0, 0)),
            ],
            out_specs=pl.BlockSpec((1, deep, 3 * hidden), lambda i, me: (i, 0, 0)),
        ),
        out_shape=of((parts, deep, 3 * hidden), BF),
        name="weight_grads", compiler_params=room(51), cost_estimate=cost(3 * unit, 6 * rows * width),
    )(me, xg, xg, saved)
    low, high = up(grads[2, :half]), down(grads[2, half:])

    def block(n):
        return pl.BlockSpec((1, deep, 3 * hidden), lambda i: (n, 0, 0))

    flat = fixed((deep, 3 * hidden))
    right, left = pl.pallas_call(
        add_far,
        grid=(1,),
        in_specs=[block(1), block(3), fixed((half, 3 * hidden)), fixed((half, 3 * hidden))],
        out_specs=[flat, flat],
        out_shape=[of((deep, 3 * hidden), BF)] * 2,
        name="add_far", compiler_params=room(60), cost_estimate=cost(0, 30 * deep * hidden),
    )(grads, grads, low, high)
    grad_gate, grad_up, grad_down = pl.pallas_call(
        add_last,
        grid=(1,),
        in_specs=[block(0), flat, flat],
        out_specs=[fixed((deep, hidden)), fixed((deep, hidden)), fixed((hidden, deep))],
        out_shape=[of((deep, hidden), BF), of((deep, hidden), BF), of((hidden, deep), BF)],
        name="add_last", compiler_params=room(60), cost_estimate=cost(0, 24 * deep * hidden),
    )(grads, up(right), down(left))
    back, grad_gate, grad_up, grad_down = together(back, grad_gate, grad_up, grad_down)

    mixed, grad_tokens, grad_combine = pl.pallas_call(
        part(merge, slots, experts),
        grid=(width // MERGE,),
        in_specs=[
            fixed((top, count)), fixed((3 * count, rows)), fixed((rows, count)),
            pl.BlockSpec((count, MERGE), lambda i: (0, i)),
            pl.BlockSpec((rows, MERGE), lambda i: (0, i)),
            pl.BlockSpec((rows, MERGE), lambda i: (0, i + width // MERGE)),
        ],
        out_specs=[
            pl.BlockSpec((count, MERGE), lambda i: (0, i)), pl.BlockSpec((count, MERGE), lambda i: (0, i)), fixed((top, count)),
        ],
        out_shape=[of((count, width), BF), of((count, width), BF), of((top, count), F32)],
        scratch_shapes=[pltpu.VMEM((rows, count), F32)],
        name="merge", compiler_params=room(60), cost_estimate=cost(4 * pick_flops, 5 * rows * width),
    )(ids, turned, pick, cotangent, back, back)
    return (mixed, grad_tokens, grad_combine.T, grad_gate[None], grad_up[None], grad_down[None])


def solution(mesh):
    rows = P(("dp", "expert"), None)
    deep, wide = P("expert", "dp", None), P("expert", None, "dp")
    return jax.shard_map(
        on_device,
        mesh=mesh,
        in_specs=(rows, rows, rows, rows, P(), deep, deep, wide),
        out_specs=(rows, rows, rows, deep, deep, wide),
        check_vma=False,
    )
```

```python
import functools

import jax
import jax.numpy as jnp
from jax import lax
from jax.experimental import pallas as pl
from jax.experimental.pallas import tpu as pltpu
from jax.sharding import PartitionSpec as P

MIB = 2**20
BF = jnp.bfloat16
F32 = jnp.float32
STEP = 512
MERGE = 2048


def contract(left, right, left_dim, right_dim):
    return lax.dot_general(
        left, right, (((left_dim,), (right_dim,)), ((), ())), preferred_element_type=F32
    )


def together(*arrays):
    return lax.optimization_barrier(arrays)


def hits(ids_ref, cap_ref, slots):
    top, count = ids_ref.shape
    experts = cap_ref.shape[1]
    numbers = lax.broadcasted_iota(jnp.int32, (experts, count), 0)
    chosen = [ids_ref[k : k + 1, :] == numbers for k in range(top)]
    taken = sum(c.astype(F32) for c in chosen)
    earlier = (
        lax.broadcasted_iota(jnp.int32, (count, count), 0)
        < lax.broadcasted_iota(jnp.int32, (count, count), 1)
    ).astype(BF)
    rank = contract(taken.astype(BF), earlier, 1, 0)
    same = lax.broadcasted_iota(jnp.int32, (experts, experts), 0) == lax.broadcasted_iota(
        jnp.int32, (experts, experts), 1
    )
    limit = jnp.sum(jnp.where(same, cap_ref[...].astype(F32), 0.0), axis=1, keepdims=True)
    slot_of = jnp.where((taken > 0.5) & (rank < limit), rank, -1.0)
    wanted = lax.broadcasted_iota(jnp.int32, (experts, slots, count), 1).astype(F32)
    held = (jnp.broadcast_to(slot_of[:, None, :], (experts, slots, count)) == wanted).astype(F32)
    return held.reshape(experts * slots, count), chosen


def shares(held, chosen, comb_ref, slots):
    weights = sum(jnp.where(c, comb_ref[k : k + 1, :], 0.0) for k, c in enumerate(chosen))
    experts, count = weights.shape
    spread = jnp.broadcast_to(weights[:, None, :], (experts, slots, count)).reshape(experts * slots, count)
    return held * spread


def pick_rows(slots, ids_ref, cap_ref, comb_ref, tokens_ref, cot_ref, out_ref, pick_ref, shares_ref, scale_ref):
    i = pl.program_id(0)
    steps = pl.num_programs(0)

    @pl.when(i == 0)
    def _():
        held, chosen = hits(ids_ref, cap_ref, slots)
        pick_ref[...] = held.astype(BF)
        share = shares(held, chosen, comb_ref, slots)
        count = share.shape[1]
        shares_ref[:, :count] = share.astype(BF)
        shares_ref[:, count:] = (share - share.astype(BF).astype(F32)).astype(BF)
        scale = jnp.sum(share, axis=1, keepdims=True)
        scale_ref[...] = jnp.broadcast_to(scale, scale_ref.shape)

    wide = out_ref.shape[1]

    @pl.when(i < steps // 2)
    def _():
        for c in range(0, wide, STEP):
            out_ref[:, c : c + STEP] = contract(pick_ref[...], tokens_ref[:, c : c + STEP], 1, 0).astype(BF)

    @pl.when(i >= steps // 2)
    def _():
        scale = scale_ref[:, :1]
        for c in range(0, wide, STEP):
            rows = contract(pick_ref[...], cot_ref[:, c : c + STEP], 1, 0)
            out_ref[:, c : c + STEP] = (scale * rows).astype(BF)


def lay_weights(gate_ref, up_ref, down_ref, pick_ref, both_ref, out_ref, turned_ref):
    count = pick_ref.shape[1]
    turned_ref[:count, :] = pick_ref[...].T
    turned_ref[count:, :] = both_ref[...].T
    hidden = gate_ref.shape[1]
    out_ref[:, :hidden] = gate_ref[...]
    out_ref[:, hidden : 2 * hidden] = up_ref[...]
    out_ref[:, 2 * hidden :] = down_ref[...].T


def expert_math(
    me_ref, xg_hbm, own_hbm, next_hbm, far_low_ref, far_high_ref, prev_hbm, od_hbm, saved_ref, xg_ref, w_ref, od_ref, in_sems, w_sems, out_sems
):
    deep, hidden = own_hbm.shape
    hidden //= 3
    parts = od_ref.shape[1] // (2 * deep)
    half = deep // 2
    order = (2, 0, 1, 3)

    def lanes(n):
        block = lax.rem(me_ref[0] + n % parts, parts) + n // parts * parts
        return pl.ds(pl.multiple_of(block * deep, deep), deep)

    def arrive(n):
        return pltpu.make_async_copy(xg_hbm.at[:, lanes(n)], xg_ref.at[:, pl.ds(n * deep, deep)], in_sems.at[n])

    def leave(n):
        return pltpu.make_async_copy(od_ref.at[:, pl.ds(n * deep, deep)], od_hbm.at[:, lanes(n)], out_sems.at[n])

    places = {0: 0, 1: 1, 3: 2}
    sources = {0: own_hbm, 1: next_hbm, 3: prev_hbm}
    moved = {n: pltpu.make_async_copy(sources[n], w_ref.at[p], w_sems.at[p]) for n, p in places.items()}

    def pieces(n):
        if n == 2:
            return [(0, far_low_ref), (half, far_high_ref)]
        return [(0, w_ref.at[places[n]])]

    for n in order:
        arrive(n).start()
        if n in moved:
            moved[n].start()
    for n in order:
        arrive(parts + n).start()
    hu = da = 0.0
    for n in order:
        arrive(n).wait()
        if n in moved:
            moved[n].wait()
        for start, w in pieces(n):
            at = n * deep + start
            hu = hu + contract(xg_ref[:, at : at + w.shape[0]], w[:, : 2 * hidden], 1, 0)
    h, u = hu[:, :hidden], hu[:, hidden:]
    s = jax.nn.sigmoid(h)
    a = (h * s * u).astype(BF)
    saved_ref[:, 2 * hidden :] = a
    for n in order:
        for start, w in pieces(n):
            at = n * deep + start
            od_ref[:, at : at + w.shape[0]] = contract(a, w[:, 2 * hidden :], 1, 1).astype(BF)
        leave(n).start()
    for n in order:
        arrive(parts + n).wait()
        for start, w in pieces(n):
            at = (parts + n) * deep + start
            da = da + contract(xg_ref[:, at : at + w.shape[0]], w[:, 2 * hidden :], 1, 0)
    dh = (da * u * s * (1.0 + h * (1.0 - s))).astype(BF)
    du = (da * h * s).astype(BF)
    saved_ref[:, :hidden] = dh
    saved_ref[:, hidden : 2 * hidden] = du
    both = jnp.concatenate([dh, du], axis=1)
    for n in order:
        m = parts + n
        for start, w in pieces(n):
            at = m * deep + start
            od_ref[:, at : at + w.shape[0]] = contract(both, w[:, : 2 * hidden], 1, 1).astype(BF)
        leave(m).start()
    for n in range(2 * parts):
        leave(n).wait()


def weight_grads(me_ref, x_ref, g_ref, saved_ref, out_ref):
    hidden = out_ref.shape[2] // 3
    out_ref[0, :, : 2 * hidden] = contract(x_ref[...], saved_ref[:, : 2 * hidden], 0, 0).astype(BF)
    out_ref[0, :, 2 * hidden :] = contract(g_ref[...], saved_ref[:, 2 * hidden :], 0, 0).astype(BF)


def add_far(next_ref, prev_ref, low_ref, high_ref, right_ref, left_ref):
    half = low_ref.shape[0]
    right_ref[:half, :] = (next_ref[0, :half, :].astype(F32) + low_ref[...].astype(F32)).astype(BF)
    right_ref[half:, :] = next_ref[0, half:, :]
    left_ref[:half, :] = prev_ref[0, :half, :]
    left_ref[half:, :] = (prev_ref[0, half:, :].astype(F32) + high_ref[...].astype(F32)).astype(BF)


def add_last(own_ref, below_ref, above_ref, gate_ref, up_ref, down_ref):
    hidden = gate_ref.shape[1]
    total = own_ref[0].astype(F32) + below_ref[...].astype(F32) + above_ref[...].astype(F32)
    gate_ref[...] = total[:, :hidden].astype(BF)
    up_ref[...] = total[:, hidden : 2 * hidden].astype(BF)
    down_ref[...] = total[:, 2 * hidden :].astype(BF).T


def merge(
    slots, experts, ids_ref, tables_ref, pick_ref, cot_ref, o_ref, d_ref, mixed_ref, rows_ref, gc_ref, dots_ref
):
    i = pl.program_id(0)

    @pl.when(i == 0)
    def _():
        dots_ref[...] = jnp.zeros(dots_ref.shape, F32)

    o = o_ref[...]
    count = ids_ref.shape[1]
    both = contract(tables_ref[count:, :], o, 1, 0)
    mixed_ref[...] = (both[:count] + both[count:]).astype(BF)
    rows_ref[...] = contract(tables_ref[:count, :], d_ref[...], 1, 0).astype(BF)
    dots_ref[...] += contract(o, cot_ref[...], 1, 1)

    @pl.when(i == pl.num_programs(0) - 1)
    def _():
        top, count = ids_ref.shape
        found = dots_ref[...] * pick_ref[...].astype(F32)
        per_expert = jnp.sum(found.reshape(experts, slots, count), axis=1)
        numbers = lax.broadcasted_iota(jnp.int32, (experts, count), 0)
        for k in range(top):
            hit = ids_ref[k : k + 1, :] == numbers
            gc_ref[k : k + 1, :] = jnp.sum(jnp.where(hit, per_expert, 0.0), axis=0, keepdims=True)


def on_device(tokens, cotangent, expert_ids, combine, capacity, w_gate, w_up, w_down):
    part = functools.partial
    of = jax.ShapeDtypeStruct
    peers = lax.axis_size("expert")
    count, width = tokens.shape
    top = expert_ids.shape[1]
    experts = capacity.shape[0]
    slots = count * top // (2 * peers)
    rows = experts * slots
    hidden = w_gate.shape[2]
    limits = capacity.reshape(1, experts)
    ids, comb = expert_ids.T, combine.T
    unit = 2 * rows * width * hidden
    pick_flops = 2 * rows * count * width

    def cost(flops, moved):
        return pl.CostEstimate(flops=flops, bytes_accessed=moved, transcendentals=0)

    def room(mib):
        return pltpu.CompilerParams(vmem_limit_bytes=mib * MIB)

    def fixed(shape):
        return pl.BlockSpec(shape, lambda i: (0,) * len(shape))

    def exchange(x):
        x = x.reshape(peers, slots, 2 * width)
        return lax.all_to_all(x, "expert", 0, 0, tiled=True).reshape(rows, 2 * width)

    block = width
    sent, pick, both = pl.pallas_call(
        part(pick_rows, slots),
        grid=(2,),
        in_specs=[
            fixed((top, count)), fixed((1, experts)), fixed((top, count)),
            pl.BlockSpec((count, block), lambda i: (0, 0)),
            pl.BlockSpec((count, block), lambda i: (0, 0)),
        ],
        out_specs=[pl.BlockSpec((rows, block), lambda i: (0, i)), fixed((rows, count)), fixed((rows, 2 * count))],
        out_shape=[of((rows, 2 * width), BF), of((rows, count), BF), of((rows, 2 * count), BF)],
        scratch_shapes=[pltpu.VMEM((rows, 128), F32)],
        name="pick_rows", compiler_params=room(60), cost_estimate=cost(2 * pick_flops, 5 * rows * width),
    )(ids, limits, comb, tokens, cotangent)
    xg = exchange(sent)

    parts = lax.axis_size("dp")
    deep = width // parts
    half = deep // 2
    me = lax.axis_index("dp").astype(jnp.int32).reshape(1)

    def up(x):
        return lax.ppermute(x, "dp", [(i, (i + 1) % parts) for i in range(parts)])

    def down(x):
        return lax.ppermute(x, "dp", [(i, (i - 1) % parts) for i in range(parts)])

    own, turned = pl.pallas_call(
        lay_weights, out_shape=[of((deep, 3 * hidden), BF), of((3 * count, rows), BF)], name="lay_weights", compiler_params=room(60),
        cost_estimate=cost(0, 12 * deep * hidden),
    )(w_gate[0], w_up[0], w_down[0], pick, both)
    before, after = up(own), down(own)
    far_low, far_high = up(before[:half]), down(after[half:])

    whole = pl.BlockSpec(memory_space=pl.ANY)
    vmem = pl.BlockSpec(memory_space=pltpu.VMEM)
    od, saved = pl.pallas_call(
        expert_math,
        in_specs=[pl.BlockSpec(memory_space=pltpu.SMEM), whole, whole, whole, vmem, vmem, whole],
        out_specs=[whole, vmem],
        out_shape=[of((rows, 2 * width), BF), of((rows, 3 * hidden), BF)],
        scratch_shapes=[
            pltpu.VMEM((rows, 2 * width), BF), pltpu.VMEM((3, deep, 3 * hidden), BF), pltpu.VMEM((rows, 2 * width), BF),
            pltpu.SemaphoreType.DMA((2 * parts,)), pltpu.SemaphoreType.DMA((3,)), pltpu.SemaphoreType.DMA((2 * parts,)),
        ],
        name="expert_math", compiler_params=room(51), cost_estimate=cost(6 * unit, 10 * rows * width),
    )(me, xg, own, after, far_low, far_high, before)
    back = exchange(od)

    grads = pl.pallas_call(
        weight_grads,
        grid_spec=pltpu.PrefetchScalarGridSpec(
            num_scalar_prefetch=1,
            grid=(parts,),
            in_specs=[
                pl.BlockSpec((rows, deep), lambda i, me: (0, lax.rem(me[0] + i, parts))),
                pl.BlockSpec((rows, deep), lambda i, me: (0, lax.rem(me[0] + i, parts) + parts)),
                pl.BlockSpec((rows, 3 * hidden), lambda i, me: (0, 0)),
            ],
            out_specs=pl.BlockSpec((1, deep, 3 * hidden), lambda i, me: (i, 0, 0)),
        ),
        out_shape=of((parts, deep, 3 * hidden), BF),
        name="weight_grads", compiler_params=room(51), cost_estimate=cost(3 * unit, 6 * rows * width),
    )(me, xg, xg, saved)
    low, high = up(grads[2, :half]), down(grads[2, half:])

    def block(n):
        return pl.BlockSpec((1, deep, 3 * hidden), lambda i: (n, 0, 0))

    flat = fixed((deep, 3 * hidden))
    right, left = pl.pallas_call(
        add_far,
        grid=(1,),
        in_specs=[block(1), block(3), fixed((half, 3 * hidden)), fixed((half, 3 * hidden))],
        out_specs=[flat, flat],
        out_shape=[of((deep, 3 * hidden), BF)] * 2,
        name="add_far", compiler_params=room(60), cost_estimate=cost(0, 30 * deep * hidden),
    )(grads, grads, low, high)
    grad_gate, grad_up, grad_down = pl.pallas_call(
        add_last,
        grid=(1,),
        in_specs=[block(0), flat, flat],
        out_specs=[fixed((deep, hidden)), fixed((deep, hidden)), fixed((hidden, deep))],
        out_shape=[of((deep, hidden), BF), of((deep, hidden), BF), of((hidden, deep), BF)],
        name="add_last", compiler_params=room(60), cost_estimate=cost(0, 24 * deep * hidden),
    )(grads, up(right), down(left))
    back, grad_gate, grad_up, grad_down = together(back, grad_gate, grad_up, grad_down)

    mixed, grad_tokens, grad_combine = pl.pallas_call(
        part(merge, slots, experts),
        grid=(width // MERGE,),
        in_specs=[
            fixed((top, count)), fixed((3 * count, rows)), fixed((rows, count)),
            pl.BlockSpec((count, MERGE), lambda i: (0, i)),
            pl.BlockSpec((rows, MERGE), lambda i: (0, i)),
            pl.BlockSpec((rows, MERGE), lambda i: (0, i + width // MERGE)),
        ],
        out_specs=[
            pl.BlockSpec((count, MERGE), lambda i: (0, i)), pl.BlockSpec((count, MERGE), lambda i: (0, i)), fixed((top, count)),
        ],
        out_shape=[of((count, width), BF), of((count, width), BF), of((top, count), F32)],
        scratch_shapes=[pltpu.VMEM((rows, count), F32)],
        name="merge", compiler_params=room(60), cost_estimate=cost(4 * pick_flops, 5 * rows * width),
    )(ids, turned, pick, cotangent, back, back)
    return (mixed, grad_tokens, grad_combine.T, grad_gate[None], grad_up[None], grad_down[None])


def solution(mesh):
    rows = P(("dp", "expert"), None)
    deep, wide = P("expert", "dp", None), P("expert", None, "dp")
    return jax.shard_map(
        on_device,
        mesh=mesh,
        in_specs=(rows, rows, rows, rows, P(), deep, deep, wide),
        out_specs=(rows, rows, rows, deep, deep, wide),
        check_vma=False,
    )
```
